512 devices in a mesh: head: 16 (over y, core), req: 32 (over x, z).
Axes of the slice: x: 4, y: 8, z: 8, core: 2. Of those that a mesh axis runs over, the one named last changes fastest.
Arguments:
- tokens: bfloat16 [4, 96, 8192], P(None, 'head', 'req'), may hold values from -6 to 6
- gate_inner_weight: bfloat16 [8192, 2, 16384], P('req', None, 'head'), may hold values from -0.0625 to 0.0625
- step_weight: bfloat16 [8192, 256], P('req', 'head'), may hold values from -0.0625 to 0.0625
- bc_weight: bfloat16 [8192, 2048], P('req', 'head'), may hold values from -0.0625 to 0.0625
- conv_inner: bfloat16 [96, 3, 16384], P('req', None, 'head'), may hold values from -6 to 6
- conv_groups: bfloat16 [96, 3, 2048], P('req', None, 'head'), may hold values from -6 to 6
- inner_taps: float32 [4, 16384], P(None, 'head'), may hold values from -0.6 to 0.6
- inner_bias: float32 [16384], P('head'), may hold values from -0.5 to 0.5
- group_taps: float32 [4, 2048], P(None, 'head'), may hold values from -0.6 to 0.6
- group_bias: float32 [2048], P('head'), may hold values from -0.5 to 0.5
- step_bias: float32 [256], P('head'), may hold values from -3 to 0
- log_decay: float32 [256], P('head'), may hold values from -2 to 1.5
- skip_gain: float32 [256], P('head'), may hold values from 0.5 to 1.5
- norm_gain: float32 [16384], P('head'), may hold values from 0.5 to 1.5
- out_weight: bfloat16 [16384, 8192], P('head', 'req'), may hold values from -0.046875 to 0.046875
- ssm_state: float32 [96, 256, 64, 128], P('req', 'head'), may hold values from -6 to 6
Outputs:
- mixed: bfloat16 [4, 96, 8192], P(None, 'head', 'req')
- new_state: float32 [96, 256, 64, 128], P('req', 'head')
- new_conv_inner: bfloat16 [96, 3, 16384], P('req', None, 'head')
- new_conv_groups: bfloat16 [96, 3, 2048], P('req', None, 'head')
The draws below stay inside these ranges and needn't reach their ends.
All inputs are finite; a program needn't handle non-finite values.
Results may differ from the reference program's by a relative error of at most 0.02.
Values may be sent and summed in bfloat16 or wider, within the bound.
No kernel may reach another device: no remote copies, remote signals or barrier semaphores. Data moves between devices by JAX's collectives and lax.ppermute only.
A program may use at most 64 MiB of HBM per device.

```python
import jax
import jax.numpy as jnp
from jax import lax

D = 8192
H = 256
P_SIZE = 64
N = 128
G = 8
KERNEL = 4
STEPS = 4
DI = 16384
REQ = 96


def level_of(rng, dims, cuts, smallest, top_value):
    def one(axis_at, blocks):
        draws = jax.random.uniform(jax.random.fold_in(jax.random.fold_in(rng, 6), axis_at), (blocks,), jnp.float32, smallest / len(cuts), top_value / len(cuts))
        return jnp.repeat(jnp.exp(draws), dims[axis_at] // blocks).reshape((-1,) + (1,) * (len(dims) - axis_at - 1))

    factor_of = one(*cuts[0])
    for cut in cuts[1:]:
        factor_of = factor_of * one(*cut)
    return factor_of


def noise(rng, shape, scale, limit, split=(), kind=jnp.bfloat16):
    level = level_of(rng, shape, split, -0.22, 0.18) if split else 1.0
    values = jax.random.normal(rng, shape, jnp.float32) * scale * level
    return jnp.minimum(jnp.maximum(values, -limit), limit).astype(kind)


def setup_inputs(seed: int = 0) -> dict:
    key_list = jax.random.split(jax.random.key(seed), 17)
    return {
        "tokens": noise(key_list[0], (STEPS, REQ, D), 1.0, 6.0, ((1, 16), (2, 32))),
        "gate_inner_weight": noise(key_list[1], (D, 2, DI), D ** -0.5, 0.0625, ((0, 32), (2, 16))),
        "step_weight": noise(key_list[2], (D, H), D ** -0.5, 0.0625, ((0, 32), (1, 16))),
        "bc_weight": noise(key_list[3], (D, 2 * G * N), D ** -0.5, 0.0625, ((0, 32), (1, 16))),
        "conv_inner": noise(key_list[4], (REQ, KERNEL - 1, DI), 1.0, 6.0, ((0, 32), (2, 16))),
        "conv_groups": noise(key_list[5], (REQ, KERNEL - 1, 2 * G * N), 1.0, 6.0, ((0, 32), (2, 16))),
        "inner_taps": jnp.clip(jax.random.uniform(key_list[6], (KERNEL, DI), jnp.float32, -0.6, 0.6) * level_of(key_list[6], (KERNEL, DI), ((1, 16),), -0.4, 0.0), -0.6, 0.6),
        "inner_bias": jnp.clip(jax.random.uniform(key_list[7], (DI,), jnp.float32, -0.5, 0.5) * level_of(key_list[7], (DI,), ((0, 16),), -0.4, 0.0), -0.5, 0.5),
        "group_taps": jnp.clip(jax.random.uniform(key_list[8], (KERNEL, 2 * G * N), jnp.float32, -0.6, 0.6) * level_of(key_list[8], (KERNEL, 2 * G * N), ((1, 16),), -0.4, 0.0), -0.6, 0.6),
        "group_bias": jnp.clip(jax.random.uniform(key_list[9], (2 * G * N,), jnp.float32, -0.5, 0.5) * level_of(key_list[9], (2 * G * N,), ((0, 16),), -0.4, 0.0), -0.5, 0.5),
        "step_bias": jnp.clip(-3.0 + 3.0 * jax.random.uniform(key_list[10], (H,), jnp.float32) ** level_of(key_list[10], (H,), ((0, 16),), -0.2, 0.2), -3.0, 0.0),
        "log_decay": jnp.clip(-2.0 + 3.5 * jax.random.uniform(key_list[11], (H,), jnp.float32) ** level_of(key_list[11], (H,), ((0, 16),), -0.2, 0.2), -2.0, 1.5),
        "skip_gain": jnp.clip(0.5 + 1.0 * jax.random.uniform(key_list[12], (H,), jnp.float32) ** level_of(key_list[12], (H,), ((0, 16),), -0.2, 0.2), 0.5, 1.5),
        "norm_gain": jnp.clip(1.0 + 0.1 * jax.random.normal(key_list[13], (DI,), jnp.float32), 0.5, 1.5),
        "out_weight": noise(key_list[14], (DI, D), DI ** -0.5, 0.046875, ((0, 16), (1, 32))),
        "ssm_state": noise(key_list[15], (REQ, H, P_SIZE, N), 1.0, 6.0, ((0, 32), (1, 16)), jnp.float32),
    }


epsilon = 1e-05

def conv_run(history, projected, taps, bias):
    step_count = projected.shape[0]
    sequence = jnp.concatenate([jnp.transpose(history, (1, 0, 2)), projected], axis=0)
    wide = sequence.astype(jnp.float32)
    summed = taps[0] * wide[0:step_count]
    for tap_num in range(1, taps.shape[0]):
        summed = summed + taps[tap_num] * wide[tap_num:tap_num + step_count]
    result = jax.nn.silu(summed + bias)
    kept = sequence[step_count:]
    return (result, jnp.transpose(kept, (1, 0, 2)))

def reference(tokens, gate_inner_weight, step_weight, bc_weight, conv_inner, conv_groups, inner_taps, inner_bias, group_taps, group_bias, step_bias, log_decay, skip_gain, norm_gain, out_weight, ssm_state):
    flat_tokens = tokens.reshape(STEPS * REQ, D)
    gate_inner = jnp.dot(flat_tokens, gate_inner_weight.reshape(D, 2 * DI), preferred_element_type=jnp.float32).astype(jnp.bfloat16).reshape(STEPS, REQ, 2, DI)
    step_proj = jnp.dot(flat_tokens, step_weight, preferred_element_type=jnp.float32).astype(jnp.bfloat16).reshape(STEPS, REQ, H)
    bc_proj = jnp.dot(flat_tokens, bc_weight, preferred_element_type=jnp.float32).astype(jnp.bfloat16).reshape(STEPS, REQ, 2 * G * N)
    x_conv, new_conv_inner = conv_run(conv_inner, gate_inner[:, :, 1], inner_taps, inner_bias)
    bc_conv, new_conv_groups = conv_run(conv_groups, bc_proj, group_taps, group_bias)
    step_size = jax.nn.softplus(step_proj.astype(jnp.float32) + step_bias)
    decay_rate = jnp.exp(-step_size * jnp.exp(log_decay))
    heads_group = H // G

    def one_request(inputs):
        current, gate_rows, inner_rows, group_rows, sizes, rates = inputs
        normed_rows = []
        for step_num in range(STEPS):
            x_step = inner_rows[step_num].reshape(H, P_SIZE)
            group_split = group_rows[step_num].reshape(G, 2, N)
            b_heads = jnp.repeat(group_split[:, 0], heads_group, axis=0)
            c_heads = jnp.repeat(group_split[:, 1], heads_group, axis=0)
            current = rates[step_num][:, None, None] * current + (sizes[step_num][:, None] * x_step)[:, :, None] * b_heads[:, None, :]
            y_heads = jnp.einsum('hpn,hn->hp', current, c_heads, precision=lax.Precision.HIGHEST) + skip_gain[:, None] * x_step
            gated_y = y_heads * jax.nn.silu(gate_rows[step_num].reshape(H, P_SIZE).astype(jnp.float32))
            grouped = gated_y.reshape(G, DI // G)
            mean_sq = lax.optimization_barrier(jnp.mean(grouped * grouped, axis=-1))
            normed = ((grouped * lax.rsqrt(mean_sq + epsilon)[:, None]).reshape(DI) * norm_gain).astype(jnp.bfloat16)
            normed_rows.append(normed)
        return (current, jnp.stack(normed_rows))
    inputs = (ssm_state, jnp.transpose(gate_inner[:, :, 0], (1, 0, 2)), jnp.transpose(x_conv, (1, 0, 2)), jnp.transpose(bc_conv, (1, 0, 2)), jnp.transpose(step_size, (1, 0, 2)), jnp.transpose(decay_rate, (1, 0, 2)))
    new_state, normed_all = lax.map(one_request, inputs)
    flat_normed = jnp.transpose(normed_all, (1, 0, 2)).reshape(STEPS * REQ, DI)
    mixed = jnp.dot(flat_normed, out_weight, preferred_element_type=jnp.float32).astype(jnp.bfloat16).reshape(STEPS, REQ, D)
    return (mixed, new_state, new_conv_inner, new_conv_groups)
```

```python
import functools

import jax
import jax.numpy as jnp
from jax import lax
from jax.experimental import pallas as pl
from jax.experimental.pallas import tpu as pltpu
from jax.sharding import Mesh
from jax.sharding import PartitionSpec as P

EPSILON = 1e-05
F32 = jnp.float32
BF16 = jnp.bfloat16
Y_SIZE, CORE_SIZE, X_SIZE, Z_SIZE = 8, 2, 4, 8
HEAD_AXES = ("y", "core")
REQ_AXES = ("x", "z")
VMEM_LIMIT = 40 * 1024 * 1024


def silu(value):
    return value / (1.0 + jnp.exp(-value))


def call(body, out_shape, scratch=(), cost=None):
    whole = pl.BlockSpec(memory_space=pltpu.VMEM)
    return pl.pallas_call(
        body,
        out_shape=out_shape,
        out_specs=jax.tree.map(lambda _: whole, out_shape),
        scratch_shapes=list(scratch),
        compiler_params=pltpu.CompilerParams(vmem_limit_bytes=VMEM_LIMIT),
        cost_estimate=cost,
    )


def fold_x(in_ref, out_ref, sums):
    parts, rows, width = in_ref.shape
    half = width // 2
    block = rows // Z_SIZE
    total = in_ref[0].astype(F32)
    for part in range(1, parts):
        total = total + in_ref[part].astype(F32)
    for z in range(Z_SIZE):
        for side in range(2):
            at = (2 * z + side) * block
            sums[at : at + block, :] = total[z * block : (z + 1) * block, side * half : (side + 1) * half]
    out_ref[...] = sums[...].astype(BF16)


def conv_steps(seq, taps, bias, steps):
    summed = taps[0:1, :] * seq[0:steps]
    for tap in range(1, taps.shape[0]):
        summed = summed + taps[tap : tap + 1, :] * seq[tap : tap + steps]
    return silu(summed + bias)


def fold_z(in_ref, hist_ref, taps_ref, bias_ref, proj_ref, bc_ref, kept_ref, seq):
    parts = in_ref.shape[0]
    requests, history, width = hist_ref.shape
    rows = in_ref.shape[1] // 2
    steps = rows // requests
    first = in_ref.shape[2] - width
    total = in_ref[0].astype(F32)
    for part in range(1, parts):
        total = total + in_ref[part].astype(F32)
    proj_ref[...] = total.astype(BF16).astype(F32)
    for req in range(requests):
        seq[0:history, :] = hist_ref[req].astype(F32)
        seq[history : history + steps, :] = proj_ref[req * steps : (req + 1) * steps, first:]
        bc_ref[req * steps : (req + 1) * steps, :] = conv_steps(seq, taps_ref[...], bias_ref[...], steps)
        kept_ref[req] = seq[steps : steps + history, :].astype(BF16)


def scan_steps(
    proj_ref,
    pair_ref,
    hist_ref,
    taps_ref,
    bias_ref,
    step_bias_ref,
    log_decay_ref,
    skip_ref,
    state_ref,
    gated_ref,
    squares_ref,
    new_state_ref,
    kept_ref,
    seq,
    spread,
    rank,
    base,
):
    requests, width, state_size = state_ref.shape
    heads = step_bias_ref.shape[1]
    history = hist_ref.shape[1]
    rows = gated_ref.shape[0]
    steps = rows // requests
    step = proj_ref[rows : 2 * rows, width : width + heads] + step_bias_ref[...]
    step_size = jnp.maximum(step, 0.0) + jnp.log1p(jnp.exp(-jnp.abs(step)))
    spread[0:rows, :] = step_size
    spread[rows : 2 * rows, :] = jnp.exp(-step_size * jnp.exp(log_decay_ref[...]))
    spread[2 * rows : 2 * rows + 1, :] = skip_ref[...]
    spread[2 * rows + 1 :, :] = jnp.zeros((spread.shape[0] - 2 * rows - 1, heads), F32)
    per_head = width // heads
    channel = lax.broadcasted_iota(jnp.int32, (heads, width), 1)
    low = lax.broadcasted_iota(jnp.int32, (heads, width), 0) * per_head
    owner = jnp.where((channel >= low) & (channel < low + per_head), 1.0, 0.0).astype(F32)
    wide = jnp.dot(spread[...], owner, precision=lax.Precision.HIGHEST, preferred_element_type=F32)
    skip = wide[2 * rows : 2 * rows + 1]
    for req in range(requests):
        start = req * steps
        seq[0:history, :] = hist_ref[req].astype(F32)
        seq[history : history + steps, :] = proj_ref[rows + start : rows + start + steps, 0:width]
        x_conv = conv_steps(seq, taps_ref[...], bias_ref[...], steps)
        kept_ref[req] = seq[steps : steps + history, :].astype(BF16)
        b_rows = pair_ref[0, start : start + steps, :]
        c_rows = pair_ref[1, start : start + steps, :]
        state = state_ref[req]
        c_high = c_rows.astype(BF16).astype(F32)
        rank[0:steps, 0:state_size] = c_high
        rank[steps : 2 * steps, 0:state_size] = c_rows - c_high
        rank[2 * steps :, 0:state_size] = jnp.zeros((rank.shape[0] - 2 * steps, state_size), F32)
        c_parts = rank[:, 0:state_size].astype(BF16)
        state_high = state.astype(BF16)
        state_low = (state - state_high.astype(F32)).astype(BF16)
        across = (((1,), (1,)), ((), ()))
        by_high = lax.dot_general(c_parts, state_high, across, preferred_element_type=F32)
        by_low = lax.dot_general(c_parts, state_low, across, preferred_element_type=F32)
        base[...] = by_high[0:steps] + by_high[steps : 2 * steps] + by_low[0:steps]
        taken = []
        fade = None
        for step_num in range(steps):
            row = start + step_num
            x_row = x_conv[step_num : step_num + 1]
            decay = wide[rows + row : rows + row + 1]
            fade = decay if fade is None else fade * decay
            taken = [(source, decay * value) for source, value in taken]
            taken.append((step_num, wide[row : row + 1] * x_row))
            y_row = fade * base[step_num : step_num + 1, :] + skip * x_row
            for source, value in taken:
                match = jnp.sum(
                    b_rows[source : source + 1] * c_rows[step_num : step_num + 1], axis=1, keepdims=True
                )
                y_row = y_row + match * value
            gated = y_row * silu(proj_ref[row : row + 1, 0:width])
            gated_ref[row : row + 1, :] = gated
            square = jnp.sum(gated * gated, axis=1, keepdims=True)
            squares_ref[row : row + 1, :] = jnp.broadcast_to(square, (1, squares_ref.shape[1]))
        b_high = b_rows.astype(BF16).astype(F32)
        b_low = b_rows - b_high
        ones = jnp.ones((steps, state_size), F32)
        zeros = jnp.zeros((steps, state_size), F32)
        rank[0:steps, 0:state_size] = b_high
        rank[steps : 2 * steps, 0:state_size] = b_high
        rank[2 * steps : 3 * steps, 0:state_size] = b_low
        rank[3 * steps :, 0:state_size] = zeros
        rank[0:steps, state_size:] = zeros
        rank[steps : 2 * steps, state_size:] = zeros
        rank[2 * steps : 3 * steps, state_size:] = zeros
        rank[3 * steps :, state_size:] = ones
        right = rank[...].astype(BF16)
        for source, value in taken:
            high = value.astype(BF16).astype(F32)
            seq[source : source + 1, :] = high
            seq[steps + source : steps + source + 1, :] = value - high
            seq[2 * steps + source : 2 * steps + source + 1, :] = high
        fade_high = fade.astype(BF16).astype(F32)
        fade_mid = (fade - fade_high).astype(BF16).astype(F32)
        seq[3 * steps : 3 * steps + 1, :] = fade_high
        seq[3 * steps + 1 : 3 * steps + 2, :] = fade_mid
        seq[3 * steps + 2 : 3 * steps + 3, :] = fade - fade_high - fade_mid
        seq[3 * steps + 3 :, :] = jnp.zeros((seq.shape[0] - 3 * steps - 3, width), F32)
        left = seq[...].astype(BF16)
        both = lax.dot_general(left, right, (((0,), (0,)), ((), ())), preferred_element_type=F32)
        new_state_ref[req] = both[:, state_size:] * state + both[:, 0:state_size]


def normalise(group_width, gated_ref, squares_ref, gain_ref, out_ref, rows_two):
    rows, width = gated_ref.shape
    half = width // 2
    mean = (squares_ref[0] + squares_ref[1])[:, 0:1] / group_width
    normed = gated_ref[...] * lax.rsqrt(mean + EPSILON) * gain_ref[...]
    rows_two[0:rows, :] = normed[:, 0:half]
    rows_two[rows : 2 * rows, :] = normed[:, half:]
    block = rows_two[...].astype(BF16)
    for copy in range(out_ref.shape[0]):
        out_ref[copy] = block


def project_out(in_ref, weight_ref, out_ref, first, second, sums):
    blocks, block_rows, half = in_ref.shape
    rows = block_rows // 2
    flat = in_ref[...].reshape(blocks * block_rows, half)
    first[...] = jnp.dot(flat, weight_ref[0:half, :], preferred_element_type=F32)
    second[...] = jnp.dot(flat, weight_ref[half:, :], preferred_element_type=F32)
    for block in range(blocks):
        at = block * block_rows
        sums[block * rows : (block + 1) * rows, :] = (
            first[at : at + rows, :] + second[at + rows : at + block_rows, :]
        )
    out_ref[...] = sums[...].astype(BF16)


def shards(
    tokens,
    gate_inner_weight,
    step_weight,
    bc_weight,
    conv_inner,
    conv_groups,
    inner_taps,
    inner_bias,
    group_taps,
    group_bias,
    step_bias,
    log_decay,
    skip_gain,
    norm_gain,
    out_weight,
    ssm_state,
):
    steps, rows_head, features = tokens.shape
    requests, heads, head_size, state_size = ssm_state.shape
    width = heads * head_size
    head_count = Y_SIZE * CORE_SIZE
    req_count = X_SIZE * Z_SIZE
    rows = steps * requests
    sds = jax.ShapeDtypeStruct

    with jax.named_scope("weights"):
        weights = jnp.concatenate(
            [
                gate_inner_weight[:, 0],
                bc_weight,
                gate_inner_weight[:, 1],
                step_weight,
                jnp.zeros((features, bc_weight.shape[1] - heads), BF16),
            ],
            axis=1,
        )
    columns = weights.shape[1]
    half = columns // 2

    with jax.named_scope("gather_tokens"):
        own = jnp.transpose(tokens, (1, 0, 2)).reshape(rows_head * steps, features)
        own = jnp.broadcast_to(own[None], (head_count,) + own.shape)
        gathered = lax.all_to_all(own, HEAD_AXES, 0, 0, tiled=True)
        gathered = gathered.reshape(req_count * rows, features)

    with jax.named_scope("project"):
        partial_proj = jnp.dot(gathered, weights, preferred_element_type=F32).astype(BF16)
        partial_proj = partial_proj.reshape(X_SIZE, Z_SIZE * rows, columns)
    with jax.named_scope("sum_x"):
        parts = lax.all_to_all(partial_proj, "x", 0, 0, tiled=True)
        folded = call(
            fold_x,
            sds((Z_SIZE * 2 * rows, half), BF16),
            [pltpu.VMEM((Z_SIZE * 2 * rows, half), F32)],
        )(parts)
    with jax.named_scope("sum_z"):
        parts = lax.all_to_all(folded.reshape(Z_SIZE, 2 * rows, half), "z", 0, 0, tiled=True)
        history = conv_groups.shape[1]
        proj, bc_conv, new_conv_groups = call(
            fold_z,
            (
                sds((2 * rows, half), F32),
                sds((rows, bc_weight.shape[1]), F32),
                sds(conv_groups.shape, BF16),
            ),
            [pltpu.VMEM((8, bc_weight.shape[1]), F32)],
        )(parts, conv_groups, group_taps, group_bias[None])
    with jax.named_scope("scan"):
        pair = lax.all_gather(bc_conv, "core", axis=0, tiled=False)
        gated, squares, new_state, new_conv_inner = call(
            scan_steps,
            (
                sds((rows, width), F32),
                sds((rows, 128), F32),
                sds((requests, width, state_size), F32),
                sds(conv_inner.shape, BF16),
            ),
            [
                pltpu.VMEM((4 * steps, width), F32),
                pltpu.VMEM((32, heads), F32),
                pltpu.VMEM((4 * steps, 2 * state_size), F32),
                pltpu.VMEM((steps, width), F32),
            ],
        )(
            proj,
            pair,
            conv_inner,
            inner_taps,
            inner_bias[None],
            step_bias[None],
            log_decay[None],
            skip_gain[None],
            ssm_state.reshape(requests, width, state_size),
        )
    with jax.named_scope("normalise"):
        squares_pair = lax.all_gather(squares, "core", axis=0, tiled=False)
        normed = call(
            functools.partial(normalise, CORE_SIZE * width),
            sds((req_count, 2 * rows, width // 2), BF16),
            [pltpu.VMEM((2 * rows, width // 2), F32)],
        )(gated, squares_pair, norm_gain[None])
    with jax.named_scope("gather_normed"):
        all_rows = lax.all_to_all(normed, REQ_AXES, 0, 0, tiled=True)
    with jax.named_scope("project_out"):
        out_columns = out_weight.shape[1]
        product = call(
            project_out,
            sds((req_count * rows, out_columns), BF16),
            [
                pltpu.VMEM((req_count * 2 * rows, out_columns), F32),
                pltpu.VMEM((req_count * 2 * rows, out_columns), F32),
                pltpu.VMEM((req_count * rows, out_columns), F32),
            ],
        )(all_rows, out_weight)
    with jax.named_scope("sum_head"):
        blocks = product.reshape(head_count, rows_head * steps, out_columns)
        blocks = lax.all_to_all(blocks, HEAD_AXES, 0, 0, tiled=True)
        mixed = jnp.sum(blocks.astype(F32), axis=0).astype(BF16)
        mixed = jnp.transpose(mixed.reshape(rows_head, steps, out_columns), (1, 0, 2))
    return (mixed, new_state.reshape(ssm_state.shape), new_conv_inner, new_conv_groups)


def solution(mesh):
    head, req = HEAD_AXES, REQ_AXES
    split = Mesh(
        mesh.devices.reshape(Y_SIZE, CORE_SIZE, X_SIZE, Z_SIZE), HEAD_AXES + REQ_AXES
    )
    placed = (
        P(None, head, req),
        P(req, None, head),
        P(req, head),
        P(req, head),
        P(req, None, head),
        P(req, None, head),
        P(None, head),
        P(head),
        P(None, head),
        P(head),
        P(head),
        P(head),
        P(head),
        P(head),
        P(head, req),
        P(req, head, None, None),
    )
    return jax.shard_map(
        shards,
        mesh=split,
        in_specs=placed,
        out_specs=(
            P(None, head, req),
            P(req, head, None, None),
            P(req, None, head),
            P(req, None, head),
        ),
        check_vma=False,
    )
```

```python
import functools

import jax
import jax.numpy as jnp
from jax import lax
from jax.experimental import pallas as pl
from jax.experimental.pallas import tpu as pltpu
from jax.sharding import Mesh
from jax.sharding import PartitionSpec as P

EPSILON = 1e-05
F32 = jnp.float32
BF16 = jnp.bfloat16
Y_SIZE, CORE_SIZE, X_SIZE, Z_SIZE = 8, 2, 4, 8
HEAD_AXES = ("y", "core")
REQ_AXES = ("x", "z")
VMEM_LIMIT = 40 * 1024 * 1024


def silu(value):
    return value / (1.0 + jnp.exp(-value))


def call(body, out_shape, scratch=(), cost=None):
    whole = pl.BlockSpec(memory_space=pltpu.VMEM)
    return pl.pallas_call(
        body,
        out_shape=out_shape,
        out_specs=jax.tree.map(lambda _: whole, out_shape),
        scratch_shapes=list(scratch),
        compiler_params=pltpu.CompilerParams(vmem_limit_bytes=VMEM_LIMIT),
        cost_estimate=cost,
    )


def project(
    x_ref, rows_ref, own_ref, first_ref, second_ref, third_ref, extra_ref, out_ref, messages
):
    cores, per_core, block_rows, features = rows_ref.shape
    y_count = per_core // X_SIZE
    rows = block_rows // 2
    lanes = out_ref.shape[1]
    tiles = out_ref.shape[0] // (X_SIZE * Z_SIZE * rows)
    here = x_ref[0]
    for core in range(cores):
        total = None
        for shift, weight_ref in enumerate((own_ref, first_ref, second_ref, third_ref)):
            source = lax.rem(here - shift + X_SIZE, X_SIZE)
            block = rows_ref[core, pl.ds(source * y_count, y_count)]
            block = block.reshape(y_count * block_rows, features)
            part = jnp.dot(block, weight_ref[...], preferred_element_type=F32)
            total = part if total is None else total + part
            if shift == 0:
                extra = jnp.dot(block, extra_ref[...], preferred_element_type=F32)
        for y in range(y_count):
            for side in range(2):
                target = 2 * (y * cores + core) + side
                at = y * block_rows + side * rows
                for tile in range(tiles):
                    value, column = total, tile * lanes
                    if column >= total.shape[1]:
                        value, column = extra, column - total.shape[1]
                    to = (target * tiles + tile) * rows
                    messages[to : to + rows, :] = value[at : at + rows, column : column + lanes]
    out_ref[...] = messages[...].astype(BF16)


def conv_steps(seq, taps, bias, steps):
    summed = taps[0:1, :] * seq[0:steps]
    for tap in range(1, taps.shape[0]):
        summed = summed + taps[tap : tap + 1, :] * seq[tap : tap + steps]
    return silu(summed + bias)


def fold(
    in_ref, hist_ref, taps_ref, bias_ref, gate_ref, inner_ref, step_ref, bc_ref, kept_ref, seq
):
    requests, history, lanes = hist_ref.shape
    rows = gate_ref.shape[0]
    steps = rows // requests
    chunk = gate_ref.shape[1] // X_SIZE
    tiles = chunk // lanes
    extra = None
    for x in range(X_SIZE):
        total = in_ref[x * Z_SIZE].astype(F32)
        for z in range(1, Z_SIZE):
            total = total + in_ref[x * Z_SIZE + z].astype(F32)
        rounded = total.astype(BF16).astype(F32)
        for tile in range(tiles):
            column = x * chunk + tile * lanes
            gate_ref[:, column : column + lanes] = rounded[tile * rows : (tile + 1) * rows]
            at = (tiles + tile) * rows
            inner_ref[:, column : column + lanes] = rounded[at : at + rows]
        part = total[2 * tiles * rows :]
        extra = part if extra is None else extra + part
    extra = extra.astype(BF16).astype(F32)
    step_ref[...] = extra[rows : 2 * rows]
    for req in range(requests):
        seq[0:history, :] = hist_ref[req].astype(F32)
        seq[history : history + steps, :] = extra[req * steps : (req + 1) * steps]
        bc_ref[req * steps : (req + 1) * steps, :] = conv_steps(seq, taps_ref[...], bias_ref[...], steps)
        kept_ref[req] = seq[steps : steps + history, :].astype(BF16)


def scan_steps(
    gate_ref,
    inner_ref,
    step_ref,
    pair_ref,
    hist_ref,
    taps_ref,
    bias_ref,
    step_bias_ref,
    log_decay_ref,
    skip_ref,
    state_ref,
    gated_ref,
    squares_ref,
    new_state_ref,
    kept_ref,
    seq,
    spread,
    rank,
    base,
):
    requests, width, state_size = state_ref.shape
    heads = step_bias_ref.shape[1]
    history = hist_ref.shape[1]
    rows = gated_ref.shape[0]
    steps = rows // requests
    step = step_ref[:, 0:heads] + step_bias_ref[...]
    step_size = jnp.maximum(step, 0.0) + jnp.log1p(jnp.exp(-jnp.abs(step)))
    spread[0:rows, :] = step_size
    spread[rows : 2 * rows, :] = jnp.exp(-step_size * jnp.exp(log_decay_ref[...]))
    spread[2 * rows : 2 * rows + 1, :] = skip_ref[...]
    spread[2 * rows + 1 :, :] = jnp.zeros((spread.shape[0] - 2 * rows - 1, heads), F32)
    per_head = width // heads
    channel = lax.broadcasted_iota(jnp.int32, (heads, width), 1)
    low = lax.broadcasted_iota(jnp.int32, (heads, width), 0) * per_head
    owner = jnp.where((channel >= low) & (channel < low + per_head), 1.0, 0.0).astype(F32)
    wide = jnp.dot(spread[...], owner, precision=lax.Precision.HIGHEST, preferred_element_type=F32)
    skip = wide[2 * rows : 2 * rows + 1]
    for req in range(requests):
        start = req * steps
        seq[0:history, :] = hist_ref[req].astype(F32)
        seq[history : history + steps, :] = inner_ref[start : start + steps, :]
        x_conv = conv_steps(seq, taps_ref[...], bias_ref[...], steps)
        kept_ref[req] = seq[steps : steps + history, :].astype(BF16)
        b_rows = pair_ref[0, start : start + steps, :]
        c_rows = pair_ref[1, start : start + steps, :]
        state = state_ref[req]
        c_high = c_rows.astype(BF16).astype(F32)
        rank[0:steps, 0:state_size] = c_high
        rank[steps : 2 * steps, 0:state_size] = c_rows - c_high
        rank[2 * steps :, 0:state_size] = jnp.zeros((rank.shape[0] - 2 * steps, state_size), F32)
        c_parts = rank[:, 0:state_size].astype(BF16)
        state_high = state.astype(BF16)
        state_low = (state - state_high.astype(F32)).astype(BF16)
        across = (((1,), (1,)), ((), ()))
        by_high = lax.dot_general(c_parts, state_high, across, preferred_element_type=F32)
        by_low = lax.dot_general(c_parts, state_low, across, preferred_element_type=F32)
        base[...] = by_high[0:steps] + by_high[steps : 2 * steps] + by_low[0:steps]
        taken = []
        fade = None
        for step_num in range(steps):
            row = start + step_num
            x_row = x_conv[step_num : step_num + 1]
            decay = wide[rows + row : rows + row + 1]
            fade = decay if fade is None else fade * decay
            taken = [(source, decay * value) for source, value in taken]
            taken.append((step_num, wide[row : row + 1] * x_row))
            y_row = fade * base[step_num : step_num + 1, :] + skip * x_row
            for source, value in taken:
                match = jnp.sum(
                    b_rows[source : source + 1] * c_rows[step_num : step_num + 1], axis=1, keepdims=True
                )
                y_row = y_row + match * value
            gated = y_row * silu(gate_ref[row : row + 1, :])
            gated_ref[row : row + 1, :] = gated
            square = jnp.sum(gated * gated, axis=1, keepdims=True)
            squares_ref[row : row + 1, :] = jnp.broadcast_to(square, (1, squares_ref.shape[1]))
        b_high = b_rows.astype(BF16).astype(F32)
        b_low = b_rows - b_high
        ones = jnp.ones((steps, state_size), F32)
        zeros = jnp.zeros((steps, state_size), F32)
        rank[0:steps, 0:state_size] = b_high
        rank[steps : 2 * steps, 0:state_size] = b_high
        rank[2 * steps : 3 * steps, 0:state_size] = b_low
        rank[3 * steps :, 0:state_size] = zeros
        rank[0:steps, state_size:] = zeros
        rank[steps : 2 * steps, state_size:] = zeros
        rank[2 * steps : 3 * steps, state_size:] = zeros
        rank[3 * steps :, state_size:] = ones
        right = rank[...].astype(BF16)
        for source, value in taken:
            high = value.astype(BF16).astype(F32)
            seq[source : source + 1, :] = high
            seq[steps + source : steps + source + 1, :] = value - high
            seq[2 * steps + source : 2 * steps + source + 1, :] = high
        fade_high = fade.astype(BF16).astype(F32)
        fade_mid = (fade - fade_high).astype(BF16).astype(F32)
        seq[3 * steps : 3 * steps + 1, :] = fade_high
        seq[3 * steps + 1 : 3 * steps + 2, :] = fade_mid
        seq[3 * steps + 2 : 3 * steps + 3, :] = fade - fade_high - fade_mid
        seq[3 * steps + 3 :, :] = jnp.zeros((seq.shape[0] - 3 * steps - 3, width), F32)
        left = seq[...].astype(BF16)
        both = lax.dot_general(left, right, (((0,), (0,)), ((), ())), preferred_element_type=F32)
        new_state_ref[req] = both[:, state_size:] * state + both[:, 0:state_size]


def normalise(group_width, gated_ref, squares_ref, gain_ref, out_ref, rows_two):
    rows, width = gated_ref.shape
    half = width // 2
    mean = (squares_ref[0] + squares_ref[1])[:, 0:1] / group_width
    normed = gated_ref[...] * lax.rsqrt(mean + EPSILON) * gain_ref[...]
    rows_two[0:rows, :] = normed[:, 0:half]
    rows_two[rows : 2 * rows, :] = normed[:, half:]
    block = rows_two[...].astype(BF16)
    for copy in range(out_ref.shape[0]):
        out_ref[copy] = block


def project_out(in_ref, weight_ref, out_ref, first, second, sums):
    blocks, block_rows, half = in_ref.shape
    rows = block_rows // 2
    flat = in_ref[...].reshape(blocks * block_rows, half)
    first[...] = jnp.dot(flat, weight_ref[0:half, :], preferred_element_type=F32)
    second[...] = jnp.dot(flat, weight_ref[half:, :], preferred_element_type=F32)
    for block in range(blocks):
        at = block * block_rows
        sums[block * rows : (block + 1) * rows, :] = (
            first[at : at + rows, :] + second[at + rows : at + block_rows, :]
        )
    out_ref[...] = sums[...].astype(BF16)


def shards(
    tokens,
    gate_inner_weight,
    step_weight,
    bc_weight,
    conv_inner,
    conv_groups,
    inner_taps,
    inner_bias,
    group_taps,
    group_bias,
    step_bias,
    log_decay,
    skip_gain,
    norm_gain,
    out_weight,
    ssm_state,
):
    steps, rows_head, features = tokens.shape
    requests, heads, head_size, state_size = ssm_state.shape
    width = heads * head_size
    head_count = Y_SIZE * CORE_SIZE
    req_count = X_SIZE * Z_SIZE
    rows = steps * requests
    sds = jax.ShapeDtypeStruct

    lanes = bc_weight.shape[1]
    chunk = width // X_SIZE
    with jax.named_scope("move_weights"):
        here = lax.axis_index("x")
        chunks = []
        for shift in range(X_SIZE):
            target = lax.rem(here + shift, X_SIZE)
            part = lax.dynamic_slice(
                gate_inner_weight, (0, 0, target * chunk), (features, 2, chunk)
            )
            if shift:
                route = [(x, (x + shift) % X_SIZE) for x in range(X_SIZE)]
                part = lax.ppermute(part, "x", route)
            chunks.append(part.reshape(features, 2 * chunk))
        extra = jnp.concatenate(
            [bc_weight, step_weight, jnp.zeros((features, lanes - heads), BF16)], axis=1
        )

    with jax.named_scope("gather_tokens"):
        own = jnp.transpose(tokens, (1, 0, 2)).reshape(rows_head * steps, features)
        own = jnp.broadcast_to(own[None], (X_SIZE * Y_SIZE,) + own.shape)
        gathered = lax.all_to_all(own, ("x", "y"), 0, 0, tiled=True)
        gathered = lax.all_gather(gathered, "core", axis=0, tiled=False)

    with jax.named_scope("project"):
        tiles = 2 * chunk // lanes + 2
        message_rows = req_count * tiles * rows
        whole = pl.BlockSpec(memory_space=pltpu.VMEM)
        messages = pl.pallas_call(
            project,
            out_shape=sds((message_rows, lanes), BF16),
            in_specs=[pl.BlockSpec(memory_space=pltpu.SMEM)] + [whole] * 6,
            out_specs=whole,
            scratch_shapes=[pltpu.VMEM((message_rows, lanes), F32)],
            compiler_params=pltpu.CompilerParams(vmem_limit_bytes=VMEM_LIMIT),
        )(here.astype(jnp.int32).reshape(1), gathered, *chunks, extra)
    with jax.named_scope("sum_req"):
        parts = lax.all_to_all(
            messages.reshape(req_count, tiles * rows, lanes), REQ_AXES, 0, 0, tiled=True
        )
        gate, inner, step, bc_conv, new_conv_groups = call(
            fold,
            (
                sds((rows, width), F32),
                sds((rows, width), F32),
                sds((rows, lanes), F32),
                sds((rows, lanes), F32),
                sds(conv_groups.shape, BF16),
            ),
            [pltpu.VMEM((8, lanes), F32)],
        )(parts, conv_groups, group_taps, group_bias[None])
    with jax.named_scope("scan"):
        pair = lax.all_gather(bc_conv, "core", axis=0, tiled=False)
        gated, squares, new_state, new_conv_inner = call(
            scan_steps,
            (
                sds((rows, width), F32),
                sds((rows, 128), F32),
                sds((requests, width, state_size), F32),
                sds(conv_inner.shape, BF16),
            ),
            [
                pltpu.VMEM((4 * steps, width), F32),
                pltpu.VMEM((32, heads), F32),
                pltpu.VMEM((4 * steps, 2 * state_size), F32),
                pltpu.VMEM((steps, width), F32),
            ],
        )(
            gate,
            inner,
            step,
            pair,
            conv_inner,
            inner_taps,
            inner_bias[None],
            step_bias[None],
            log_decay[None],
            skip_gain[None],
            ssm_state.reshape(requests, width, state_size),
        )
    with jax.named_scope("normalise"):
        squares_pair = lax.all_gather(squares, "core", axis=0, tiled=False)
        normed = call(
            functools.partial(normalise, CORE_SIZE * width),
            sds((req_count, 2 * rows, width // 2), BF16),
            [pltpu.VMEM((2 * rows, width // 2), F32)],
        )(gated, squares_pair, norm_gain[None])
    with jax.named_scope("gather_normed"):
        all_rows = lax.all_to_all(normed, REQ_AXES, 0, 0, tiled=True)
    with jax.named_scope("project_out"):
        out_columns = out_weight.shape[1]
        product = call(
            project_out,
            sds((req_count * rows, out_columns), BF16),
            [
                pltpu.VMEM((req_count * 2 * rows, out_columns), F32),
                pltpu.VMEM((req_count * 2 * rows, out_columns), F32),
                pltpu.VMEM((req_count * rows, out_columns), F32),
            ],
        )(all_rows, out_weight)
    with jax.named_scope("sum_head"):
        blocks = product.reshape(head_count, rows_head * steps, out_columns)
        blocks = lax.all_to_all(blocks, HEAD_AXES, 0, 0, tiled=True)
        mixed = jnp.sum(blocks.astype(F32), axis=0).astype(BF16)
        mixed = jnp.transpose(mixed.reshape(rows_head, steps, out_columns), (1, 0, 2))
    return (mixed, new_state.reshape(ssm_state.shape), new_conv_inner, new_conv_groups)


def solution(mesh):
    head, req = HEAD_AXES, REQ_AXES
    split = Mesh(
        mesh.devices.reshape(Y_SIZE, CORE_SIZE, X_SIZE, Z_SIZE), HEAD_AXES + REQ_AXES
    )
    placed = (
        P(None, head, req),
        P(req, None, head),
        P(req, head),
        P(req, head),
        P(req, None, head),
        P(req, None, head),
        P(None, head),
        P(head),
        P(None, head),
        P(head),
        P(head),
        P(head),
        P(head),
        P(head),
        P(head, req),
        P(req, head, None, None),
    )
    return jax.shard_map(
        shards,
        mesh=split,
        in_specs=placed,
        out_specs=(
            P(None, head, req),
            P(req, head, None, None),
            P(req, None, head),
            P(req, None, head),
        ),
        check_vma=False,
    )
```

```python
import functools

import jax
import jax.numpy as jnp
from jax import lax
from jax.experimental import pallas as pl
from jax.experimental.pallas import tpu as pltpu
from jax.sharding import Mesh
from jax.sharding import PartitionSpec as P

EPSILON = 1e-05
F32 = jnp.float32
BF16 = jnp.bfloat16
Y_SIZE, CORE_SIZE = 8, 2
HEAD_AXES = ("y", "core")
REQ_AXES = ("x1", "x0", "z2", "z1", "z0")
REQ_COUNT = 32
SQUARE_AXES = ("x0", "z0")
SQUARE = 4
MEMBERS = [
    [16 * x1 + 8 * x0 + 2 * z_high + z0 for x1 in range(2) for z_high in range(4)]
    for x0 in range(2)
    for z0 in range(2)
]
VMEM_LIMIT = 40 * 1024 * 1024


def silu(value):
    return value / (1.0 + jnp.exp(-value))


def call(body, out_shape, scratch=(), cost=None):
    whole = pl.BlockSpec(memory_space=pltpu.VMEM)
    return pl.pallas_call(
        body,
        out_shape=out_shape,
        out_specs=jax.tree.map(lambda _: whole, out_shape),
        scratch_shapes=list(scratch),
        compiler_params=pltpu.CompilerParams(vmem_limit_bytes=VMEM_LIMIT),
        cost_estimate=cost,
    )


def copy_tokens(in_ref, out_ref, flat):
    requests, steps, _ = in_ref.shape
    for req in range(requests):
        flat[req * steps : (req + 1) * steps, :] = in_ref[req].astype(F32)
    block = flat[...].astype(BF16)
    for copy in range(out_ref.shape[0]):
        out_ref[copy] = block


def sum_heads(in_ref, out_ref, flat):
    requests, steps, _ = out_ref.shape
    total = in_ref[0].astype(F32)
    for part in range(1, in_ref.shape[0]):
        total = total + in_ref[part].astype(F32)
    flat[...] = total
    for req in range(requests):
        out_ref[req] = flat[req * steps : (req + 1) * steps, :].astype(BF16)


def project(
    here_ref, rows_ref, own_ref, first_ref, second_ref, third_ref, extra_ref, out_ref, messages
):
    cores, per_core, block_rows, features = rows_ref.shape
    y_count = per_core // SQUARE
    rows = block_rows // 2
    lanes = out_ref.shape[1]
    tiles = out_ref.shape[0] // (REQ_COUNT * rows)
    here = here_ref[0]
    for core in range(cores):
        total = None
        for shift, weight_ref in enumerate((own_ref, first_ref, second_ref, third_ref)):
            source = jnp.bitwise_xor(here, shift)
            block = rows_ref[core, pl.ds(source * y_count, y_count)]
            block = block.reshape(y_count * block_rows, features)
            part = jnp.dot(block, weight_ref[...], preferred_element_type=F32)
            total = part if total is None else total + part
            if shift == 0:
                extra = jnp.dot(block, extra_ref[...], preferred_element_type=F32)
        for y in range(y_count):
            for side in range(2):
                target = 2 * (y * cores + core) + side
                at = y * block_rows + side * rows
                for tile in range(tiles):
                    value, column = total, tile * lanes
                    if column >= total.shape[1]:
                        value, column = extra, column - total.shape[1]
                    to = (target * tiles + tile) * rows
                    messages[to : to + rows, :] = value[at : at + rows, column : column + lanes]
    out_ref[...] = messages[...].astype(BF16)


def conv_steps(seq, taps, bias, steps):
    summed = taps[0:1, :] * seq[0:steps]
    for tap in range(1, taps.shape[0]):
        summed = summed + taps[tap : tap + 1, :] * seq[tap : tap + steps]
    return silu(summed + bias)


def fold(
    in_ref, hist_ref, taps_ref, bias_ref, gate_ref, inner_ref, step_ref, bc_ref, kept_ref, seq
):
    requests, history, lanes = hist_ref.shape
    rows = gate_ref.shape[0]
    steps = rows // requests
    chunk = gate_ref.shape[1] // SQUARE
    tiles = chunk // lanes
    extra = None
    for square, members in enumerate(MEMBERS):
        total = in_ref[members[0]].astype(F32)
        for member in members[1:]:
            total = total + in_ref[member].astype(F32)
        rounded = total.astype(BF16).astype(F32)
        for tile in range(tiles):
            column = square * chunk + tile * lanes
            gate_ref[:, column : column + lanes] = rounded[tile * rows : (tile + 1) * rows]
            at = (tiles + tile) * rows
            inner_ref[:, column : column + lanes] = rounded[at : at + rows]
        part = total[2 * tiles * rows :]
        extra = part if extra is None else extra + part
    extra = extra.astype(BF16).astype(F32)
    step_ref[...] = extra[rows : 2 * rows]
    for req in range(requests):
        seq[0:history, :] = hist_ref[req].astype(F32)
        seq[history : history + steps, :] = extra[req * steps : (req + 1) * steps]
        bc_ref[req * steps : (req + 1) * steps, :] = conv_steps(seq, taps_ref[...], bias_ref[...], steps)
        kept_ref[req] = seq[steps : steps + history, :].astype(BF16)


def scan_steps(
    gate_ref,
    inner_ref,
    step_ref,
    pair_ref,
    hist_ref,
    taps_ref,
    bias_ref,
    step_bias_ref,
    log_decay_ref,
    skip_ref,
    state_ref,
    gated_ref,
    squares_ref,
    new_state_ref,
    kept_ref,
    seq,
    spread,
    rank,
    base,
):
    requests, width, state_size = state_ref.shape
    heads = step_bias_ref.shape[1]
    history = hist_ref.shape[1]
    rows = gated_ref.shape[0]
    steps = rows // requests
    step = step_ref[:, 0:heads] + step_bias_ref[...]
    step_size = jnp.maximum(step, 0.0) + jnp.log1p(jnp.exp(-jnp.abs(step)))
    spread[0:rows, :] = step_size
    spread[rows : 2 * rows, :] = jnp.exp(-step_size * jnp.exp(log_decay_ref[...]))
    spread[2 * rows : 2 * rows + 1, :] = skip_ref[...]
    spread[2 * rows + 1 :, :] = jnp.zeros((spread.shape[0] - 2 * rows - 1, heads), F32)
    per_head = width // heads
    channel = lax.broadcasted_iota(jnp.int32, (heads, width), 1)
    low = lax.broadcasted_iota(jnp.int32, (heads, width), 0) * per_head
    owner = jnp.where((channel >= low) & (channel < low + per_head), 1.0, 0.0).astype(F32)
    wide = jnp.dot(spread[...], owner, precision=lax.Precision.HIGHEST, preferred_element_type=F32)
    skip = wide[2 * rows : 2 * rows + 1]
    for req in range(requests):
        start = req * steps
        seq[0:history, :] = hist_ref[req].astype(F32)
        seq[history : history + steps, :] = inner_ref[start : start + steps, :]
        x_conv = conv_steps(seq, taps_ref[...], bias_ref[...], steps)
        kept_ref[req] = seq[steps : steps + history, :].astype(BF16)
        b_rows = pair_ref[0, start : start + steps, :]
        c_rows = pair_ref[1, start : start + steps, :]
        state = state_ref[req]
        c_high = c_rows.astype(BF16).astype(F32)
        rank[0:steps, 0:state_size] = c_high
        rank[steps : 2 * steps, 0:state_size] = c_rows - c_high
        rank[2 * steps :, 0:state_size] = jnp.zeros((rank.shape[0] - 2 * steps, state_size), F32)
        c_parts = rank[:, 0:state_size].astype(BF16)
        state_high = state.astype(BF16)
        state_low = (state - state_high.astype(F32)).astype(BF16)
        across = (((1,), (1,)), ((), ()))
        by_high = lax.dot_general(c_parts, state_high, across, preferred_element_type=F32)
        by_low = lax.dot_general(c_parts, state_low, across, preferred_element_type=F32)
        base[...] = by_high[0:steps] + by_high[steps : 2 * steps] + by_low[0:steps]
        taken = []
        fade = None
        for step_num in range(steps):
            row = start + step_num
            x_row = x_conv[step_num : step_num + 1]
            decay = wide[rows + row : rows + row + 1]
            fade = decay if fade is None else fade * decay
            taken = [(source, decay * value) for source, value in taken]
            taken.append((step_num, wide[row : row + 1] * x_row))
            y_row = fade * base[step_num : step_num + 1, :] + skip * x_row
            for source, value in taken:
                match = jnp.sum(
                    b_rows[source : source + 1] * c_rows[step_num : step_num + 1], axis=1, keepdims=True
                )
                y_row = y_row + match * value
            gated = y_row * silu(gate_ref[row : row + 1, :])
            gated_ref[row : row + 1, :] = gated
            square = jnp.sum(gated * gated, axis=1, keepdims=True)
            squares_ref[row : row + 1, :] = jnp.broadcast_to(square, (1, squares_ref.shape[1]))
        b_high = b_rows.astype(BF16).astype(F32)
        b_low = b_rows - b_high
        ones = jnp.ones((steps, state_size), F32)
        zeros = jnp.zeros((steps, state_size), F32)
        rank[0:steps, 0:state_size] = b_high
        rank[steps : 2 * steps, 0:state_size] = b_high
        rank[2 * steps : 3 * steps, 0:state_size] = b_low
        rank[3 * steps :, 0:state_size] = zeros
        rank[0:steps, state_size:] = zeros
        rank[steps : 2 * steps, state_size:] = zeros
        rank[2 * steps : 3 * steps, state_size:] = zeros
        rank[3 * steps :, state_size:] = ones
        right = rank[...].astype(BF16)
        for source, value in taken:
            high = value.astype(BF16).astype(F32)
            seq[source : source + 1, :] = high
            seq[steps + source : steps + source + 1, :] = value - high
            seq[2 * steps + source : 2 * steps + source + 1, :] = high
        fade_high = fade.astype(BF16).astype(F32)
        fade_mid = (fade - fade_high).astype(BF16).astype(F32)
        seq[3 * steps : 3 * steps + 1, :] = fade_high
        seq[3 * steps + 1 : 3 * steps + 2, :] = fade_mid
        seq[3 * steps + 2 : 3 * steps + 3, :] = fade - fade_high - fade_mid
        seq[3 * steps + 3 :, :] = jnp.zeros((seq.shape[0] - 3 * steps - 3, width), F32)
        left = seq[...].astype(BF16)
        both = lax.dot_general(left, right, (((0,), (0,)), ((), ())), preferred_element_type=F32)
        new_state_ref[req] = both[:, state_size:] * state + both[:, 0:state_size]


def normalise(group_width, gated_ref, squares_ref, gain_ref, out_ref, rows_two):
    rows, width = gated_ref.shape
    half = width // 2
    mean = (squares_ref[0] + squares_ref[1])[:, 0:1] / group_width
    normed = gated_ref[...] * lax.rsqrt(mean + EPSILON) * gain_ref[...]
    rows_two[0:rows, :] = normed[:, 0:half]
    rows_two[rows : 2 * rows, :] = normed[:, half:]
    block = rows_two[...].astype(BF16)
    for copy in range(out_ref.shape[0]):
        out_ref[copy] = block


def project_out(in_ref, weight_ref, out_ref, first, second, sums):
    blocks, block_rows, half = in_ref.shape
    rows = block_rows // 2
    flat = in_ref[...].reshape(blocks * block_rows, half)
    first[...] = jnp.dot(flat, weight_ref[0:half, :], preferred_element_type=F32)
    second[...] = jnp.dot(flat, weight_ref[half:, :], preferred_element_type=F32)
    for block in range(blocks):
        at = block * block_rows
        sums[block * rows : (block + 1) * rows, :] = (
            first[at : at + rows, :] + second[at + rows : at + block_rows, :]
        )
    out_ref[...] = sums[...].astype(BF16)


def shards(
    tokens,
    gate_inner_weight,
    step_weight,
    bc_weight,
    conv_inner,
    conv_groups,
    inner_taps,
    inner_bias,
    group_taps,
    group_bias,
    step_bias,
    log_decay,
    skip_gain,
    norm_gain,
    out_weight,
    ssm_state,
):
    steps, rows_head, features = tokens.shape
    requests, heads, head_size, state_size = ssm_state.shape
    width = heads * head_size
    head_count = Y_SIZE * CORE_SIZE
    req_count = REQ_COUNT
    rows = steps * requests
    sds = jax.ShapeDtypeStruct

    lanes = bc_weight.shape[1]
    chunk = width // SQUARE
    with jax.named_scope("move_weights"):
        here = lax.axis_index(SQUARE_AXES)
        chunks = []
        for flip in range(SQUARE):
            target = jnp.bitwise_xor(here, flip)
            part = lax.dynamic_slice(
                gate_inner_weight, (0, 0, target * chunk), (features, 2, chunk)
            )
            if flip:
                route = [(at, at ^ flip) for at in range(SQUARE)]
                part = lax.ppermute(part, SQUARE_AXES, route)
            chunks.append(part.reshape(features, 2 * chunk))
        extra = jnp.concatenate(
            [bc_weight, step_weight, jnp.zeros((features, lanes - heads), BF16)], axis=1
        )

    with jax.named_scope("gather_tokens"):
        own = call(
            copy_tokens,
            sds((SQUARE * Y_SIZE, rows_head * steps, features), BF16),
            [pltpu.VMEM((rows_head * steps, features), F32)],
        )(jnp.transpose(tokens, (1, 0, 2)))
        gathered = lax.all_to_all(own, SQUARE_AXES + ("y",), 0, 0, tiled=True)
        gathered = lax.all_gather(gathered, "core", axis=0, tiled=False)

    with jax.named_scope("project"):
        tiles = 2 * chunk // lanes + 2
        message_rows = req_count * tiles * rows
        whole = pl.BlockSpec(memory_space=pltpu.VMEM)
        messages = pl.pallas_call(
            project,
            out_shape=sds((message_rows, lanes), BF16),
            in_specs=[pl.BlockSpec(memory_space=pltpu.SMEM)] + [whole] * 6,
            out_specs=whole,
            scratch_shapes=[pltpu.VMEM((message_rows, lanes), F32)],
            compiler_params=pltpu.CompilerParams(vmem_limit_bytes=VMEM_LIMIT),
        )(here.astype(jnp.int32).reshape(1), gathered, *chunks, extra)
    with jax.named_scope("sum_req"):
        parts = lax.all_to_all(
            messages.reshape(req_count, tiles * rows, lanes), REQ_AXES, 0, 0, tiled=True
        )
        gate, inner, step, bc_conv, new_conv_groups = call(
            fold,
            (
                sds((rows, width), F32),
                sds((rows, width), F32),
                sds((rows, lanes), F32),
                sds((rows, lanes), F32),
                sds(conv_groups.shape, BF16),
            ),
            [pltpu.VMEM((8, lanes), F32)],
        )(parts, conv_groups, group_taps, group_bias[None])
    with jax.named_scope("scan"):
        pair = lax.all_gather(bc_conv, "core", axis=0, tiled=False)
        gated, squares, new_state, new_conv_inner = call(
            scan_steps,
            (
                sds((rows, width), F32),
                sds((rows, 128), F32),
                sds((requests, width, state_size), F32),
                sds(conv_inner.shape, BF16),
            ),
            [
                pltpu.VMEM((4 * steps, width), F32),
                pltpu.VMEM((32, heads), F32),
                pltpu.VMEM((4 * steps, 2 * state_size), F32),
                pltpu.VMEM((steps, width), F32),
            ],
        )(
            gate,
            inner,
            step,
            pair,
            conv_inner,
            inner_taps,
            inner_bias[None],
            step_bias[None],
            log_decay[None],
            skip_gain[None],
            ssm_state.reshape(requests, width, state_size),
        )
    with jax.named_scope("normalise"):
        squares_pair = lax.all_gather(squares, "core", axis=0, tiled=False)
        normed = call(
            functools.partial(normalise, CORE_SIZE * width),
            sds((req_count, 2 * rows, width // 2), BF16),
            [pltpu.VMEM((2 * rows, width // 2), F32)],
        )(gated, squares_pair, norm_gain[None])
    with jax.named_scope("gather_normed"):
        all_rows = lax.all_to_all(normed, REQ_AXES, 0, 0, tiled=True)
    with jax.named_scope("project_out"):
        out_columns = out_weight.shape[1]
        product = call(
            project_out,
            sds((req_count * rows, out_columns), BF16),
            [
                pltpu.VMEM((req_count * 2 * rows, out_columns), F32),
                pltpu.VMEM((req_count * 2 * rows, out_columns), F32),
                pltpu.VMEM((req_count * rows, out_columns), F32),
            ],
        )(all_rows, out_weight)
    with jax.named_scope("sum_head"):
        blocks = product.reshape(head_count, rows_head * steps, out_columns)
        blocks = lax.all_to_all(blocks, HEAD_AXES, 0, 0, tiled=True)
        mixed = call(
            sum_heads,
            sds((rows_head, steps, out_columns), BF16),
            [pltpu.VMEM((rows_head * steps, out_columns), F32)],
        )(blocks)
        mixed = jnp.transpose(mixed, (1, 0, 2))
    return (mixed, new_state.reshape(ssm_state.shape), new_conv_inner, new_conv_groups)


def solution(mesh):
    head, req = HEAD_AXES, REQ_AXES
    split = Mesh(
        mesh.devices.reshape((Y_SIZE, CORE_SIZE) + (2,) * len(REQ_AXES)), HEAD_AXES + REQ_AXES
    )
    placed = (
        P(None, head, req),
        P(req, None, head),
        P(req, head),
        P(req, head),
        P(req, None, head),
        P(req, None, head),
        P(None, head),
        P(head),
        P(None, head),
        P(head),
        P(head),
        P(head),
        P(head),
        P(head),
        P(head, req),
        P(req, head, None, None),
    )
    return jax.shard_map(
        shards,
        mesh=split,
        in_specs=placed,
        out_specs=(
            P(None, head, req),
            P(req, head, None, None),
            P(req, None, head),
            P(req, None, head),
        ),
        check_vma=False,
    )
```

```python
import functools

import jax
import jax.numpy as jnp
from jax import lax
from jax.experimental import pallas as pl
from jax.experimental.pallas import tpu as pltpu
from jax.sharding import Mesh
from jax.sharding import PartitionSpec as P

EPSILON = 1e-05
F32 = jnp.float32
BF16 = jnp.bfloat16
Y_SIZE, CORE_SIZE = 8, 2
HEAD_AXES = ("y", "core")
REQ_AXES = ("x1", "x0", "z2", "z1", "z0")
REQ_COUNT = 32
SQUARE_AXES = ("x0", "z0")
SQUARE = 4
PAIR_AXIS = "z0"
REST_AXES = ("x1", "x0", "z2", "z1")
REST = 16
MEMBERS = [
    [16 * x1 + 8 * x0 + 2 * z_high + z0 for x1 in range(2) for z_high in range(4)]
    for x0 in range(2)
    for z0 in range(2)
]
VMEM_LIMIT = 40 * 1024 * 1024


def silu(value):
    return value / (1.0 + jnp.exp(-value))


WHOLE = pl.BlockSpec(memory_space=pltpu.VMEM)
SCALARS = pl.BlockSpec(memory_space=pltpu.SMEM)


def call(body, out_shape, scratch=(), in_specs=None):
    places = {} if in_specs is None else {"in_specs": in_specs}
    return pl.pallas_call(
        body,
        out_shape=out_shape,
        out_specs=jax.tree.map(lambda _: WHOLE, out_shape),
        scratch_shapes=list(scratch),
        compiler_params=pltpu.CompilerParams(vmem_limit_bytes=VMEM_LIMIT),
        **places,
    )


def copy_tokens(in_ref, out_ref, flat):
    requests, steps, _ = in_ref.shape
    for req in range(requests):
        flat[req * steps : (req + 1) * steps, :] = in_ref[req].astype(F32)
    block = flat[...].astype(BF16)
    for copy in range(out_ref.shape[0]):
        out_ref[copy] = block


def sum_heads(in_ref, out_ref):
    requests, steps, _ = out_ref.shape
    lanes = in_ref.shape[2]
    half = requests // 2
    for side in range(2):
        total = in_ref[side].astype(F32)
        for part in range(2 + side, in_ref.shape[0], 2):
            total = total + in_ref[part].astype(F32)
        for req in range(half):
            left, right = req * steps, (half + req) * steps
            out_ref[side * half + req, :, 0:lanes] = total[left : left + steps].astype(BF16)
            out_ref[side * half + req, :, lanes:] = total[right : right + steps].astype(BF16)


def project(
    here_ref, rows_ref, own_ref, first_ref, second_ref, third_ref, extra_ref, out_ref, messages
):
    cores, per_core, block_rows, features = rows_ref.shape
    y_count = per_core // SQUARE
    rows = block_rows // 2
    lanes = out_ref.shape[1]
    tiles = out_ref.shape[0] // (REQ_COUNT * rows)
    here = here_ref[0]
    for core in range(cores):
        total = None
        for shift, weight_ref in enumerate((own_ref, first_ref, second_ref, third_ref)):
            source = jnp.bitwise_xor(here, shift)
            block = rows_ref[core, pl.ds(source * y_count, y_count)]
            block = block.reshape(y_count * block_rows, features)
            part = jnp.dot(block, weight_ref[...], preferred_element_type=F32)
            total = part if total is None else total + part
            if shift == 0:
                extra = jnp.dot(block, extra_ref[...], preferred_element_type=F32)
        for y in range(y_count):
            for side in range(2):
                target = 2 * (y * cores + core) + side
                at = y * block_rows + side * rows
                for tile in range(tiles):
                    value, column = total, tile * lanes
                    if column >= total.shape[1]:
                        value, column = extra, column - total.shape[1]
                    to = (target * tiles + tile) * rows
                    messages[to : to + rows, :] = value[at : at + rows, column : column + lanes]
    out_ref[...] = messages[...].astype(BF16)


def conv_steps(seq, taps, bias, steps):
    summed = taps[0:1, :] * seq[0:steps]
    for tap in range(1, taps.shape[0]):
        summed = summed + taps[tap : tap + 1, :] * seq[tap : tap + steps]
    return silu(summed + bias)


def fold(
    in_ref, hist_ref, taps_ref, bias_ref, gate_ref, inner_ref, step_ref, bc_ref, kept_ref, seq
):
    requests, history, lanes = hist_ref.shape
    rows = gate_ref.shape[0]
    steps = rows // requests
    chunk = gate_ref.shape[1] // SQUARE
    tiles = chunk // lanes
    extra = None
    for square, members in enumerate(MEMBERS):
        total = in_ref[members[0]].astype(F32)
        for member in members[1:]:
            total = total + in_ref[member].astype(F32)
        rounded = total.astype(BF16).astype(F32)
        for tile in range(tiles):
            column = square * chunk + tile * lanes
            gate_ref[:, column : column + lanes] = rounded[tile * rows : (tile + 1) * rows]
            at = (tiles + tile) * rows
            inner_ref[:, column : column + lanes] = rounded[at : at + rows]
        part = total[2 * tiles * rows :]
        extra = part if extra is None else extra + part
    extra = extra.astype(BF16).astype(F32)
    step_ref[...] = extra[rows : 2 * rows]
    for req in range(requests):
        seq[0:history, :] = hist_ref[req].astype(F32)
        seq[history : history + steps, :] = extra[req * steps : (req + 1) * steps]
        bc_ref[req * steps : (req + 1) * steps, :] = conv_steps(seq, taps_ref[...], bias_ref[...], steps)
        kept_ref[req] = seq[steps : steps + history, :].astype(BF16)


def scan_steps(
    gate_ref,
    inner_ref,
    step_ref,
    pair_ref,
    hist_ref,
    taps_ref,
    bias_ref,
    step_bias_ref,
    log_decay_ref,
    skip_ref,
    state_ref,
    gated_ref,
    squares_ref,
    new_state_ref,
    kept_ref,
    seq,
    spread,
    rank,
    base,
):
    requests, width, state_size = state_ref.shape
    heads = step_bias_ref.shape[1]
    history = hist_ref.shape[1]
    rows = gated_ref.shape[0]
    steps = rows // requests
    step = step_ref[:, 0:heads] + step_bias_ref[...]
    step_size = jnp.maximum(step, 0.0) + jnp.log1p(jnp.exp(-jnp.abs(step)))
    spread[0:rows, :] = step_size
    spread[rows : 2 * rows, :] = jnp.exp(-step_size * jnp.exp(log_decay_ref[...]))
    spread[2 * rows : 2 * rows + 1, :] = skip_ref[...]
    spread[2 * rows + 1 :, :] = jnp.zeros((spread.shape[0] - 2 * rows - 1, heads), F32)
    per_head = width // heads
    channel = lax.broadcasted_iota(jnp.int32, (heads, width), 1)
    low = lax.broadcasted_iota(jnp.int32, (heads, width), 0) * per_head
    owner = jnp.where((channel >= low) & (channel < low + per_head), 1.0, 0.0).astype(F32)
    wide = jnp.dot(spread[...], owner, precision=lax.Precision.HIGHEST, preferred_element_type=F32)
    skip = wide[2 * rows : 2 * rows + 1]
    for req in range(requests):
        start = req * steps
        seq[0:history, :] = hist_ref[req].astype(F32)
        seq[history : history + steps, :] = inner_ref[start : start + steps, :]
        x_conv = conv_steps(seq, taps_ref[...], bias_ref[...], steps)
        kept_ref[req] = seq[steps : steps + history, :].astype(BF16)
        b_rows = pair_ref[0, start : start + steps, :]
        c_rows = pair_ref[1, start : start + steps, :]
        state = state_ref[req]
        c_high = c_rows.astype(BF16).astype(F32)
        rank[0:steps, 0:state_size] = c_high
        rank[steps : 2 * steps, 0:state_size] = c_rows - c_high
        rank[2 * steps :, 0:state_size] = jnp.zeros((rank.shape[0] - 2 * steps, state_size), F32)
        c_parts = rank[:, 0:state_size].astype(BF16)
        state_high = state.astype(BF16)
        state_low = (state - state_high.astype(F32)).astype(BF16)
        across = (((1,), (1,)), ((), ()))
        by_high = lax.dot_general(c_parts, state_high, across, preferred_element_type=F32)
        by_low = lax.dot_general(c_parts, state_low, across, preferred_element_type=F32)
        base[...] = by_high[0:steps] + by_high[steps : 2 * steps] + by_low[0:steps]
        taken = []
        fade = None
        for step_num in range(steps):
            row = start + step_num
            x_row = x_conv[step_num : step_num + 1]
            decay = wide[rows + row : rows + row + 1]
            fade = decay if fade is None else fade * decay
            taken = [(source, decay * value) for source, value in taken]
            taken.append((step_num, wide[row : row + 1] * x_row))
            y_row = fade * base[step_num : step_num + 1, :] + skip * x_row
            for source, value in taken:
                match = jnp.sum(
                    b_rows[source : source + 1] * c_rows[step_num : step_num + 1], axis=1, keepdims=True
                )
                y_row = y_row + match * value
            gated = y_row * silu(gate_ref[row : row + 1, :])
            gated_ref[row : row + 1, :] = gated
            square = jnp.sum(gated * gated, axis=1, keepdims=True)
            squares_ref[row : row + 1, :] = jnp.broadcast_to(square, (1, squares_ref.shape[1]))
        b_high = b_rows.astype(BF16).astype(F32)
        b_low = b_rows - b_high
        ones = jnp.ones((steps, state_size), F32)
        zeros = jnp.zeros((steps, state_size), F32)
        rank[0:steps, 0:state_size] = b_high
        rank[steps : 2 * steps, 0:state_size] = b_high
        rank[2 * steps : 3 * steps, 0:state_size] = b_low
        rank[3 * steps :, 0:state_size] = zeros
        rank[0:steps, state_size:] = zeros
        rank[steps : 2 * steps, state_size:] = zeros
        rank[2 * steps : 3 * steps, state_size:] = zeros
        rank[3 * steps :, state_size:] = ones
        right = rank[...].astype(BF16)
        for source, value in taken:
            high = value.astype(BF16).astype(F32)
            seq[source : source + 1, :] = high
            seq[steps + source : steps + source + 1, :] = value - high
            seq[2 * steps + source : 2 * steps + source + 1, :] = high
        fade_high = fade.astype(BF16).astype(F32)
        fade_mid = (fade - fade_high).astype(BF16).astype(F32)
        seq[3 * steps : 3 * steps + 1, :] = fade_high
        seq[3 * steps + 1 : 3 * steps + 2, :] = fade_mid
        seq[3 * steps + 2 : 3 * steps + 3, :] = fade - fade_high - fade_mid
        seq[3 * steps + 3 :, :] = jnp.zeros((seq.shape[0] - 3 * steps - 3, width), F32)
        left = seq[...].astype(BF16)
        both = lax.dot_general(left, right, (((0,), (0,)), ((), ())), preferred_element_type=F32)
        new_state_ref[req] = both[:, state_size:] * state + both[:, 0:state_size]


def normalise(group_width, gated_ref, squares_ref, gain_ref, out_ref, rows_two):
    rows, width = gated_ref.shape
    half = width // 2
    mean = (squares_ref[0] + squares_ref[1])[:, 0:1] / group_width
    normed = gated_ref[...] * lax.rsqrt(mean + EPSILON) * gain_ref[...]
    rows_two[0:rows, :] = normed[:, 0:half]
    rows_two[rows : 2 * rows, :] = normed[:, half:]
    block = rows_two[...].astype(BF16)
    for copy in range(out_ref.shape[0]):
        out_ref[copy] = block


def project_out(in_ref, weights_ref, out_ref, first, second, sums):
    blocks, block_rows, half = in_ref.shape
    rows = block_rows // 2
    lanes = out_ref.shape[-1]
    flat = in_ref[...].reshape(blocks * block_rows, half)
    for side in range(weights_ref.shape[0]):
        first[...] = jnp.dot(flat, weights_ref[side, 0:half, :], preferred_element_type=F32)
        second[...] = jnp.dot(flat, weights_ref[side, half:, :], preferred_element_type=F32)
        for block in range(blocks):
            at = block * block_rows
            total = first[at : at + rows, :] + second[at + rows : at + block_rows, :]
            sums[block, side, 0:rows, :] = total[:, 0:lanes]
            sums[block, side, rows : 2 * rows, :] = total[:, lanes : 2 * lanes]
    out_ref[...] = sums[...].astype(BF16)


def shards(
    tokens,
    gate_inner_weight,
    step_weight,
    bc_weight,
    conv_inner,
    conv_groups,
    inner_taps,
    inner_bias,
    group_taps,
    group_bias,
    step_bias,
    log_decay,
    skip_gain,
    norm_gain,
    out_weight,
    ssm_state,
):
    steps, rows_head, features = tokens.shape
    requests, heads, head_size, state_size = ssm_state.shape
    width = heads * head_size
    req_count = REQ_COUNT
    rows = steps * requests
    sds = jax.ShapeDtypeStruct

    lanes = bc_weight.shape[1]
    chunk = width // SQUARE
    with jax.named_scope("move_weights"):
        here = lax.axis_index(SQUARE_AXES)
        chunks = []
        for flip in range(SQUARE):
            target = jnp.bitwise_xor(here, flip)
            part = lax.dynamic_slice(
                gate_inner_weight, (0, 0, target * chunk), (features, 2, chunk)
            )
            if flip:
                route = [(at, at ^ flip) for at in range(SQUARE)]
                part = lax.ppermute(part, SQUARE_AXES, route)
            chunks.append(part.reshape(features, 2 * chunk))
        extra = jnp.concatenate(
            [bc_weight, step_weight, jnp.zeros((features, lanes - heads), BF16)], axis=1
        )

    with jax.named_scope("move_out_weight"):
        pair_weights = lax.all_gather(out_weight, PAIR_AXIS, axis=0, tiled=False)

    with jax.named_scope("gather_tokens"):
        own = call(
            copy_tokens,
            sds((SQUARE * Y_SIZE, rows_head * steps, features), BF16),
            [pltpu.VMEM((rows_head * steps, features), F32)],
        )(jnp.transpose(tokens, (1, 0, 2)))
        gathered = lax.all_to_all(own, SQUARE_AXES + ("y",), 0, 0, tiled=True)
        gathered = lax.all_gather(gathered, "core", axis=0, tiled=False)

    with jax.named_scope("project"):
        tiles = 2 * chunk // lanes + 2
        message_rows = req_count * tiles * rows
        messages = call(
            project,
            sds((message_rows, lanes), BF16),
            [pltpu.VMEM((message_rows, lanes), F32)],
            [SCALARS] + [WHOLE] * 6,
        )(here.astype(jnp.int32).reshape(1), gathered, *chunks, extra)
    with jax.named_scope("sum_req"):
        parts = lax.all_to_all(
            messages.reshape(req_count, tiles * rows, lanes), REQ_AXES, 0, 0, tiled=True
        )
        gate, inner, step, bc_conv, new_conv_groups = call(
            fold,
            (
                sds((rows, width), F32),
                sds((rows, width), F32),
                sds((rows, lanes), F32),
                sds((rows, lanes), F32),
                sds(conv_groups.shape, BF16),
            ),
            [pltpu.VMEM((8, lanes), F32)],
        )(parts, conv_groups, group_taps, group_bias[None])
    with jax.named_scope("scan"):
        pair = lax.all_gather(bc_conv, "core", axis=0, tiled=False)
        gated, squares, new_state, new_conv_inner = call(
            scan_steps,
            (
                sds((rows, width), F32),
                sds((rows, 128), F32),
                sds((requests, width, state_size), F32),
                sds(conv_inner.shape, BF16),
            ),
            [
                pltpu.VMEM((4 * steps, width), F32),
                pltpu.VMEM((32, heads), F32),
                pltpu.VMEM((4 * steps, 2 * state_size), F32),
                pltpu.VMEM((steps, width), F32),
            ],
        )(
            gate,
            inner,
            step,
            pair,
            conv_inner,
            inner_taps,
            inner_bias[None],
            step_bias[None],
            log_decay[None],
            skip_gain[None],
            ssm_state.reshape(requests, width, state_size),
        )
    with jax.named_scope("normalise"):
        squares_pair = lax.all_gather(squares, "core", axis=0, tiled=False)
        normed = call(
            functools.partial(normalise, CORE_SIZE * width),
            sds((REST, 2 * rows, width // 2), BF16),
            [pltpu.VMEM((2 * rows, width // 2), F32)],
        )(gated, squares_pair, norm_gain[None])
    with jax.named_scope("gather_normed"):
        some_rows = lax.all_to_all(normed, REST_AXES, 0, 0, tiled=True)
    with jax.named_scope("project_out"):
        out_columns = out_weight.shape[1]
        block = (REST, 2, 2 * rows, out_columns // 2)
        product = call(
            project_out,
            sds(block, BF16),
            [
                pltpu.VMEM((REST * 2 * rows, out_columns), F32),
                pltpu.VMEM((REST * 2 * rows, out_columns), F32),
                pltpu.VMEM(block, F32),
            ],
        )(some_rows, pair_weights)
    with jax.named_scope("sum_head"):
        blocks = product.reshape((2 * REST,) + block[2:])
        blocks = lax.all_to_all(blocks, HEAD_AXES + (PAIR_AXIS,), 0, 0, tiled=True)
        mixed = call(sum_heads, sds((rows_head, steps, out_columns), BF16))(blocks)
        mixed = jnp.transpose(mixed, (1, 0, 2))
    return (mixed, new_state.reshape(ssm_state.shape), new_conv_inner, new_conv_groups)


def solution(mesh):
    head, req = HEAD_AXES, REQ_AXES
    split = Mesh(
        mesh.devices.reshape((Y_SIZE, CORE_SIZE) + (2,) * len(REQ_AXES)), HEAD_AXES + REQ_AXES
    )
    placed = (
        P(None, head, req),
        P(req, None, head),
        P(req, head),
        P(req, head),
        P(req, None, head),
        P(req, None, head),
        P(None, head),
        P(head),
        P(None, head),
        P(head),
        P(head),
        P(head),
        P(head),
        P(head),
        P(head, req),
        P(req, head, None, None),
    )
    return jax.shard_map(
        shards,
        mesh=split,
        in_specs=placed,
        out_specs=(
            P(None, head, req),
            P(req, head, None, None),
            P(req, None, head),
            P(req, None, head),
        ),
        check_vma=False,
    )
```

```python
import functools

import jax
import jax.numpy as jnp
from jax import lax
from jax.experimental import pallas as pl
from jax.experimental.pallas import tpu as pltpu
from jax.sharding import Mesh
from jax.sharding import PartitionSpec as P

EPSILON = 1e-05
F32 = jnp.float32
BF16 = jnp.bfloat16
Y_SIZE, CORE_SIZE = 8, 2
HEAD_AXES = ("y", "core")
REQ_AXES = ("x1", "x0", "z2", "z1", "z0")
REQ_COUNT = 32
SQUARE_AXES = ("x0", "z0")
SQUARE = 4
PAIR_AXIS = "z0"
REST_AXES = ("x1", "x0", "z2", "z1")
REST = 16
MEMBERS = [
    [16 * x1 + 8 * x0 + 2 * z_high + z0 for x1 in range(2) for z_high in range(4)]
    for x0 in range(2)
    for z0 in range(2)
]
VMEM_LIMIT = 40 * 1024 * 1024


def silu(value):
    return value / (1.0 + jnp.exp(-value))


WHOLE = pl.BlockSpec(memory_space=pltpu.VMEM)
SCALARS = pl.BlockSpec(memory_space=pltpu.SMEM)
UNREAD = pl.BlockSpec(memory_space=pl.ANY)


def call(body, out_shape, scratch=(), in_specs=None):
    places = {} if in_specs is None else {"in_specs": in_specs}
    return pl.pallas_call(
        body,
        out_shape=out_shape,
        out_specs=jax.tree.map(lambda _: WHOLE, out_shape),
        scratch_shapes=list(scratch),
        compiler_params=pltpu.CompilerParams(vmem_limit_bytes=VMEM_LIMIT),
        **places,
    )


def copy_tokens(in_ref, _first, _second, out_ref, flat):
    requests, steps, _ = in_ref.shape
    for req in range(requests):
        flat[req * steps : (req + 1) * steps, :] = in_ref[req].astype(F32)
    block = flat[...].astype(BF16)
    for copy in range(out_ref.shape[0]):
        out_ref[copy] = block


def sum_heads(in_ref, out_ref):
    requests, steps, _ = out_ref.shape
    lanes = in_ref.shape[2]
    half = requests // 2
    for side in range(2):
        total = in_ref[side].astype(F32)
        for part in range(2 + side, in_ref.shape[0], 2):
            total = total + in_ref[part].astype(F32)
        for req in range(half):
            left, right = req * steps, (half + req) * steps
            out_ref[side * half + req, :, 0:lanes] = total[left : left + steps].astype(BF16)
            out_ref[side * half + req, :, lanes:] = total[right : right + steps].astype(BF16)


def project(
    here_ref, rows_ref, own_ref, first_ref, second_ref, third_ref, extra_ref, out_ref, messages
):
    cores, per_core, block_rows, features = rows_ref.shape
    y_count = per_core // SQUARE
    rows = block_rows // 2
    lanes = out_ref.shape[1]
    tiles = out_ref.shape[0] // (REQ_COUNT * rows)
    here = here_ref[0]
    for core in range(cores):
        total = None
        for shift, weight_ref in enumerate((own_ref, first_ref, second_ref, third_ref)):
            source = jnp.bitwise_xor(here, shift)
            block = rows_ref[core, pl.ds(source * y_count, y_count)]
            block = block.reshape(y_count * block_rows, features)
            part = jnp.dot(block, weight_ref[...], preferred_element_type=F32)
            total = part if total is None else total + part
            if shift == 0:
                extra = jnp.dot(block, extra_ref[...], preferred_element_type=F32)
        for y in range(y_count):
            for side in range(2):
                target = 2 * (y * cores + core) + side
                at = y * block_rows + side * rows
                for tile in range(tiles):
                    value, column = total, tile * lanes
                    if column >= total.shape[1]:
                        value, column = extra, column - total.shape[1]
                    to = (target * tiles + tile) * rows
                    messages[to : to + rows, :] = value[at : at + rows, column : column + lanes]
    out_ref[...] = messages[...].astype(BF16)


def conv_steps(seq, taps, bias, steps):
    summed = taps[0:1, :] * seq[0:steps]
    for tap in range(1, taps.shape[0]):
        summed = summed + taps[tap : tap + 1, :] * seq[tap : tap + steps]
    return silu(summed + bias)


def fold(
    in_ref, hist_ref, taps_ref, bias_ref, gate_ref, inner_ref, step_ref, bc_ref, kept_ref, seq
):
    requests, history, lanes = hist_ref.shape
    rows = gate_ref.shape[0]
    steps = rows // requests
    chunk = gate_ref.shape[1] // SQUARE
    tiles = chunk // lanes
    extra = None
    for square, members in enumerate(MEMBERS):
        total = in_ref[members[0]].astype(F32)
        for member in members[1:]:
            total = total + in_ref[member].astype(F32)
        rounded = total.astype(BF16).astype(F32)
        for tile in range(tiles):
            column = square * chunk + tile * lanes
            gate_ref[:, column : column + lanes] = rounded[tile * rows : (tile + 1) * rows]
            at = (tiles + tile) * rows
            inner_ref[:, column : column + lanes] = rounded[at : at + rows]
        part = total[2 * tiles * rows :]
        extra = part if extra is None else extra + part
    extra = extra.astype(BF16).astype(F32)
    step_ref[...] = extra[rows : 2 * rows]
    for req in range(requests):
        seq[0:history, :] = hist_ref[req].astype(F32)
        seq[history : history + steps, :] = extra[req * steps : (req + 1) * steps]
        bc_ref[req * steps : (req + 1) * steps, :] = conv_steps(seq, taps_ref[...], bias_ref[...], steps)
        kept_ref[req] = seq[steps : steps + history, :].astype(BF16)


def scan_steps(
    gate_ref,
    inner_ref,
    step_ref,
    pair_ref,
    hist_ref,
    taps_ref,
    bias_ref,
    step_bias_ref,
    log_decay_ref,
    skip_ref,
    state_ref,
    gated_ref,
    squares_ref,
    new_state_ref,
    kept_ref,
    seq,
    spread,
    rank,
    base,
):
    requests, width, state_size = state_ref.shape
    heads = step_bias_ref.shape[1]
    history = hist_ref.shape[1]
    rows = gated_ref.shape[0]
    steps = rows // requests
    step = step_ref[:, 0:heads] + step_bias_ref[...]
    step_size = jnp.maximum(step, 0.0) + jnp.log1p(jnp.exp(-jnp.abs(step)))
    spread[0:rows, :] = step_size
    spread[rows : 2 * rows, :] = jnp.exp(-step_size * jnp.exp(log_decay_ref[...]))
    spread[2 * rows : 2 * rows + 1, :] = skip_ref[...]
    spread[2 * rows + 1 :, :] = jnp.zeros((spread.shape[0] - 2 * rows - 1, heads), F32)
    per_head = width // heads
    channel = lax.broadcasted_iota(jnp.int32, (heads, width), 1)
    low = lax.broadcasted_iota(jnp.int32, (heads, width), 0) * per_head
    owner = jnp.where((channel >= low) & (channel < low + per_head), 1.0, 0.0).astype(F32)
    wide = jnp.dot(spread[...], owner, precision=lax.Precision.HIGHEST, preferred_element_type=F32)
    skip = wide[2 * rows : 2 * rows + 1]
    for req in range(requests):
        start = req * steps
        seq[0:history, :] = hist_ref[req].astype(F32)
        seq[history : history + steps, :] = inner_ref[start : start + steps, :]
        x_conv = conv_steps(seq, taps_ref[...], bias_ref[...], steps)
        kept_ref[req] = seq[steps : steps + history, :].astype(BF16)
        b_rows = pair_ref[0, start : start + steps, :]
        c_rows = pair_ref[1, start : start + steps, :]
        state = state_ref[req]
        c_high = c_rows.astype(BF16).astype(F32)
        rank[0:steps, 0:state_size] = c_high
        rank[steps : 2 * steps, 0:state_size] = c_rows - c_high
        rank[2 * steps :, 0:state_size] = jnp.zeros((rank.shape[0] - 2 * steps, state_size), F32)
        c_parts = rank[:, 0:state_size].astype(BF16)
        state_high = state.astype(BF16)
        state_low = (state - state_high.astype(F32)).astype(BF16)
        across = (((1,), (1,)), ((), ()))
        by_high = lax.dot_general(c_parts, state_high, across, preferred_element_type=F32)
        by_low = lax.dot_general(c_parts, state_low, across, preferred_element_type=F32)
        base[...] = by_high[0:steps] + by_high[steps : 2 * steps] + by_low[0:steps]
        taken = []
        fade = None
        for step_num in range(steps):
            row = start + step_num
            x_row = x_conv[step_num : step_num + 1]
            decay = wide[rows + row : rows + row + 1]
            fade = decay if fade is None else fade * decay
            taken = [(source, decay * value) for source, value in taken]
            taken.append((step_num, wide[row : row + 1] * x_row))
            y_row = fade * base[step_num : step_num + 1, :] + skip * x_row
            for source, value in taken:
                match = jnp.sum(
                    b_rows[source : source + 1] * c_rows[step_num : step_num + 1], axis=1, keepdims=True
                )
                y_row = y_row + match * value
            gated = y_row * silu(gate_ref[row : row + 1, :])
            gated_ref[row : row + 1, :] = gated
            square = jnp.sum(gated * gated, axis=1, keepdims=True)
            squares_ref[row : row + 1, :] = jnp.broadcast_to(square, (1, squares_ref.shape[1]))
        b_high = b_rows.astype(BF16).astype(F32)
        b_low = b_rows - b_high
        ones = jnp.ones((steps, state_size), F32)
        zeros = jnp.zeros((steps, state_size), F32)
        rank[0:steps, 0:state_size] = b_high
        rank[steps : 2 * steps, 0:state_size] = b_high
        rank[2 * steps : 3 * steps, 0:state_size] = b_low
        rank[3 * steps :, 0:state_size] = zeros
        rank[0:steps, state_size:] = zeros
        rank[steps : 2 * steps, state_size:] = zeros
        rank[2 * steps : 3 * steps, state_size:] = zeros
        rank[3 * steps :, state_size:] = ones
        right = rank[...].astype(BF16)
        for source, value in taken:
            high = value.astype(BF16).astype(F32)
            seq[source : source + 1, :] = high
            seq[steps + source : steps + source + 1, :] = value - high
            seq[2 * steps + source : 2 * steps + source + 1, :] = high
        fade_high = fade.astype(BF16).astype(F32)
        fade_mid = (fade - fade_high).astype(BF16).astype(F32)
        seq[3 * steps : 3 * steps + 1, :] = fade_high
        seq[3 * steps + 1 : 3 * steps + 2, :] = fade_mid
        seq[3 * steps + 2 : 3 * steps + 3, :] = fade - fade_high - fade_mid
        seq[3 * steps + 3 :, :] = jnp.zeros((seq.shape[0] - 3 * steps - 3, width), F32)
        left = seq[...].astype(BF16)
        both = lax.dot_general(left, right, (((0,), (0,)), ((), ())), preferred_element_type=F32)
        new_state_ref[req] = both[:, state_size:] * state + both[:, 0:state_size]


def normalise(group_width, gated_ref, squares_ref, gain_ref, _, out_ref, rows_two):
    rows, width = gated_ref.shape
    half = width // 2
    mean = (squares_ref[0] + squares_ref[1])[:, 0:1] / group_width
    normed = gated_ref[...] * lax.rsqrt(mean + EPSILON) * gain_ref[...]
    rows_two[0:rows, :] = normed[:, 0:half]
    rows_two[rows : 2 * rows, :] = normed[:, half:]
    block = rows_two[...].astype(BF16)
    for copy in range(out_ref.shape[0]):
        out_ref[copy] = block


def project_out(side_ref, in_ref, own_ref, other_ref, out_ref, first, second, sums):
    blocks, block_rows, half = in_ref.shape
    rows = block_rows // 2
    lanes = out_ref.shape[-1]
    flat = in_ref[...].reshape(blocks * block_rows, half)
    for weight_ref, side in ((own_ref, side_ref[0]), (other_ref, 1 - side_ref[0])):
        first[...] = jnp.dot(flat, weight_ref[0:half, :], preferred_element_type=F32)
        second[...] = jnp.dot(flat, weight_ref[half:, :], preferred_element_type=F32)
        for block in range(blocks):
            at = block * block_rows
            total = first[at : at + rows, :] + second[at + rows : at + block_rows, :]
            sums[block, side, 0:rows, :] = total[:, 0:lanes]
            sums[block, side, rows : 2 * rows, :] = total[:, lanes : 2 * lanes]
    out_ref[...] = sums[...].astype(BF16)


def shards(
    tokens,
    gate_inner_weight,
    step_weight,
    bc_weight,
    conv_inner,
    conv_groups,
    inner_taps,
    inner_bias,
    group_taps,
    group_bias,
    step_bias,
    log_decay,
    skip_gain,
    norm_gain,
    out_weight,
    ssm_state,
):
    steps, rows_head, features = tokens.shape
    requests, heads, head_size, state_size = ssm_state.shape
    width = heads * head_size
    req_count = REQ_COUNT
    rows = steps * requests
    sds = jax.ShapeDtypeStruct

    lanes = bc_weight.shape[1]
    chunk = width // SQUARE
    with jax.named_scope("move_weights"):
        here = lax.axis_index(SQUARE_AXES)
        chunks, moved = [], []
        for flip in range(SQUARE):
            target = jnp.bitwise_xor(here, flip)
            part = lax.dynamic_slice(
                gate_inner_weight, (0, 0, target * chunk), (features, 2, chunk)
            )
            if flip:
                route = [(at, at ^ flip) for at in range(SQUARE)]
                part = lax.ppermute(part, SQUARE_AXES, route)
                moved.append(part)
            chunks.append(part.reshape(features, 2 * chunk))
        extra = jnp.concatenate(
            [bc_weight, step_weight, jnp.zeros((features, lanes - heads), BF16)], axis=1
        )

    with jax.named_scope("move_out_weight"):
        side = lax.axis_index(PAIR_AXIS)
        other_weight = lax.ppermute(out_weight, PAIR_AXIS, [(0, 1), (1, 0)])

    with jax.named_scope("gather_tokens"):
        own = call(
            copy_tokens,
            sds((SQUARE * Y_SIZE, rows_head * steps, features), BF16),
            [pltpu.VMEM((rows_head * steps, features), F32)],
            [WHOLE, UNREAD, UNREAD],
        )(jnp.transpose(tokens, (1, 0, 2)), *moved[:2])
        gathered = lax.all_to_all(own, SQUARE_AXES + ("y",), 0, 0, tiled=True)
        gathered = lax.all_gather(gathered, "core", axis=0, tiled=False)

    with jax.named_scope("project"):
        tiles = 2 * chunk // lanes + 2
        message_rows = req_count * tiles * rows
        messages = call(
            project,
            sds((message_rows, lanes), BF16),
            [pltpu.VMEM((message_rows, lanes), F32)],
            [SCALARS] + [WHOLE] * 6,
        )(here.astype(jnp.int32).reshape(1), gathered, *chunks, extra)
    with jax.named_scope("sum_req"):
        parts = lax.all_to_all(
            messages.reshape(req_count, tiles * rows, lanes), REQ_AXES, 0, 0, tiled=True
        )
        gate, inner, step, bc_conv, new_conv_groups = call(
            fold,
            (
                sds((rows, width), F32),
                sds((rows, width), F32),
                sds((rows, lanes), F32),
                sds((rows, lanes), F32),
                sds(conv_groups.shape, BF16),
            ),
            [pltpu.VMEM((8, lanes), F32)],
        )(parts, conv_groups, group_taps, group_bias[None])
    with jax.named_scope("scan"):
        pair = lax.all_gather(bc_conv, "core", axis=0, tiled=False)
        gated, squares, new_state, new_conv_inner = call(
            scan_steps,
            (
                sds((rows, width), F32),
                sds((rows, 128), F32),
                sds((requests, width, state_size), F32),
                sds(conv_inner.shape, BF16),
            ),
            [
                pltpu.VMEM((4 * steps, width), F32),
                pltpu.VMEM((32, heads), F32),
                pltpu.VMEM((4 * steps, 2 * state_size), F32),
                pltpu.VMEM((steps, width), F32),
            ],
        )(
            gate,
            inner,
            step,
            pair,
            conv_inner,
            inner_taps,
            inner_bias[None],
            step_bias[None],
            log_decay[None],
            skip_gain[None],
            ssm_state.reshape(requests, width, state_size),
        )
    with jax.named_scope("normalise"):
        squares_pair = lax.all_gather(squares, "core", axis=0, tiled=False)
        normed = call(
            functools.partial(normalise, CORE_SIZE * width),
            sds((REST, 2 * rows, width // 2), BF16),
            [pltpu.VMEM((2 * rows, width // 2), F32)],
            [WHOLE] * 3 + [UNREAD],
        )(gated, squares_pair, norm_gain[None], other_weight)
    with jax.named_scope("gather_normed"):
        some_rows = lax.all_to_all(normed, REST_AXES, 0, 0, tiled=True)
    with jax.named_scope("project_out"):
        out_columns = out_weight.shape[1]
        block = (REST, 2, 2 * rows, out_columns // 2)
        product = call(
            project_out,
            sds(block, BF16),
            [
                pltpu.VMEM((REST * 2 * rows, out_columns), F32),
                pltpu.VMEM((REST * 2 * rows, out_columns), F32),
                pltpu.VMEM(block, F32),
            ],
            [SCALARS] + [WHOLE] * 3,
        )(side.astype(jnp.int32).reshape(1), some_rows, out_weight, other_weight)
    with jax.named_scope("sum_head"):
        blocks = product.reshape((2 * REST,) + block[2:])
        blocks = lax.all_to_all(blocks, HEAD_AXES + (PAIR_AXIS,), 0, 0, tiled=True)
        mixed = call(sum_heads, sds((rows_head, steps, out_columns), BF16))(blocks)
        mixed = jnp.transpose(mixed, (1, 0, 2))
    return (mixed, new_state.reshape(ssm_state.shape), new_conv_inner, new_conv_groups)


def solution(mesh):
    head, req = HEAD_AXES, REQ_AXES
    split = Mesh(
        mesh.devices.reshape((Y_SIZE, CORE_SIZE) + (2,) * len(REQ_AXES)), HEAD_AXES + REQ_AXES
    )
    placed = (
        P(None, head, req),
        P(req, None, head),
        P(req, head),
        P(req, head),
        P(req, None, head),
        P(req, None, head),
        P(None, head),
        P(head),
        P(None, head),
        P(head),
        P(head),
        P(head),
        P(head),
        P(head),
        P(head, req),
        P(req, head, None, None),
    )
    return jax.shard_map(
        shards,
        mesh=split,
        in_specs=placed,
        out_specs=(
            P(None, head, req),
            P(req, head, None, None),
            P(req, None, head),
            P(req, None, head),
        ),
        check_vma=False,
    )
```

```python
import functools

import jax
import jax.numpy as jnp
from jax import lax
from jax.experimental import pallas as pl
from jax.experimental.pallas import tpu as pltpu
from jax.sharding import Mesh
from jax.sharding import PartitionSpec as P

EPSILON = 1e-05
F32 = jnp.float32
BF16 = jnp.bfloat16
Y_SIZE, CORE_SIZE = 8, 2
HEAD_AXES = ("y", "core")
REQ_AXES = ("x1", "x0", "z2", "z1", "z0")
REQ_COUNT = 32
SHARE_AXIS = "x0"
SHARE = 2
MEMBERS = [[16 * x1 + 8 * x0 + z for x1 in range(2) for z in range(8)] for x0 in range(SHARE)]
PAIR_AXIS = "z0"
REST_AXES = ("x1", "x0", "z2", "z1")
REST = 16
VMEM_LIMIT = 40 * 1024 * 1024


def silu(value):
    return value / (1.0 + jnp.exp(-value))


WHOLE = pl.BlockSpec(memory_space=pltpu.VMEM)
SCALARS = pl.BlockSpec(memory_space=pltpu.SMEM)
UNREAD = pl.BlockSpec(memory_space=pl.ANY)


def call(body, out_shape, scratch=(), in_specs=None):
    places = {} if in_specs is None else {"in_specs": in_specs}
    return pl.pallas_call(
        body,
        out_shape=out_shape,
        out_specs=jax.tree.map(lambda _: WHOLE, out_shape),
        scratch_shapes=list(scratch),
        compiler_params=pltpu.CompilerParams(vmem_limit_bytes=VMEM_LIMIT),
        **places,
    )


def copy_tokens(in_ref, out_ref, flat):
    requests, steps, _ = in_ref.shape
    for req in range(requests):
        flat[req * steps : (req + 1) * steps, :] = in_ref[req].astype(F32)
    block = flat[...].astype(BF16)
    for copy in range(out_ref.shape[0]):
        out_ref[copy] = block


def sum_heads(in_ref, out_ref):
    requests, steps, _ = out_ref.shape
    lanes = in_ref.shape[2]
    half = requests // 2
    for side in range(2):
        total = in_ref[side].astype(F32)
        for part in range(2 + side, in_ref.shape[0], 2):
            total = total + in_ref[part].astype(F32)
        for req in range(half):
            left, right = req * steps, (half + req) * steps
            out_ref[side * half + req, :, 0:lanes] = total[left : left + steps].astype(BF16)
            out_ref[side * half + req, :, lanes:] = total[right : right + steps].astype(BF16)


def project(
    here_ref, rows_ref, own_ref, other_ref, extra_ref, _, out_ref, messages
):
    cores, per_core, block_rows, features = rows_ref.shape
    y_count = per_core // SHARE
    rows = block_rows // 2
    lanes = out_ref.shape[1]
    tiles = out_ref.shape[0] // (REQ_COUNT * rows)
    here = here_ref[0]
    for core in range(cores):
        total = None
        for shift, weight_ref in enumerate((own_ref, other_ref)):
            source = 1 - here if shift else here
            block = rows_ref[core, pl.ds(source * y_count, y_count)]
            block = block.reshape(y_count * block_rows, features)
            part = jnp.dot(block, weight_ref[...], preferred_element_type=F32)
            total = part if total is None else total + part
            if shift == 0:
                extra = jnp.dot(block, extra_ref[...], preferred_element_type=F32)
        for y in range(y_count):
            for side in range(2):
                target = 2 * (y * cores + core) + side
                at = y * block_rows + side * rows
                for tile in range(tiles):
                    value, column = total, tile * lanes
                    if column >= total.shape[1]:
                        value, column = extra, column - total.shape[1]
                    to = (target * tiles + tile) * rows
                    messages[to : to + rows, :] = value[at : at + rows, column : column + lanes]
    out_ref[...] = messages[...].astype(BF16)


def conv_steps(seq, taps, bias, steps):
    summed = taps[0:1, :] * seq[0:steps]
    for tap in range(1, taps.shape[0]):
        summed = summed + taps[tap : tap + 1, :] * seq[tap : tap + steps]
    return silu(summed + bias)


def fold(
    in_ref, hist_ref, taps_ref, bias_ref, gate_ref, inner_ref, step_ref, bc_ref, kept_ref, seq
):
    requests, history, lanes = hist_ref.shape
    rows = gate_ref.shape[0]
    steps = rows // requests
    chunk = gate_ref.shape[1] // SHARE
    tiles = chunk // lanes
    extra = None
    for share, members in enumerate(MEMBERS):
        total = in_ref[members[0]].astype(F32)
        for member in members[1:]:
            total = total + in_ref[member].astype(F32)
        rounded = total.astype(BF16).astype(F32)
        for tile in range(tiles):
            column = share * chunk + tile * lanes
            gate_ref[:, column : column + lanes] = rounded[tile * rows : (tile + 1) * rows]
            at = (tiles + tile) * rows
            inner_ref[:, column : column + lanes] = rounded[at : at + rows]
        part = total[2 * tiles * rows :]
        extra = part if extra is None else extra + part
    extra = extra.astype(BF16).astype(F32)
    step_ref[...] = extra[rows : 2 * rows]
    for req in range(requests):
        seq[0:history, :] = hist_ref[req].astype(F32)
        seq[history : history + steps, :] = extra[req * steps : (req + 1) * steps]
        bc_ref[req * steps : (req + 1) * steps, :] = conv_steps(seq, taps_ref[...], bias_ref[...], steps)
        kept_ref[req] = seq[steps : steps + history, :].astype(BF16)


def scan_steps(
    gate_ref,
    inner_ref,
    step_ref,
    pair_ref,
    hist_ref,
    taps_ref,
    bias_ref,
    step_bias_ref,
    log_decay_ref,
    skip_ref,
    state_ref,
    gated_ref,
    squares_ref,
    new_state_ref,
    kept_ref,
    seq,
    spread,
    rank,
    base,
):
    requests, width, state_size = state_ref.shape
    heads = step_bias_ref.shape[1]
    history = hist_ref.shape[1]
    rows = gated_ref.shape[0]
    steps = rows // requests
    step = step_ref[:, 0:heads] + step_bias_ref[...]
    step_size = jnp.maximum(step, 0.0) + jnp.log1p(jnp.exp(-jnp.abs(step)))
    spread[0:rows, :] = step_size
    spread[rows : 2 * rows, :] = jnp.exp(-step_size * jnp.exp(log_decay_ref[...]))
    spread[2 * rows : 2 * rows + 1, :] = skip_ref[...]
    spread[2 * rows + 1 :, :] = jnp.zeros((spread.shape[0] - 2 * rows - 1, heads), F32)
    per_head = width // heads
    channel = lax.broadcasted_iota(jnp.int32, (heads, width), 1)
    low = lax.broadcasted_iota(jnp.int32, (heads, width), 0) * per_head
    owner = jnp.where((channel >= low) & (channel < low + per_head), 1.0, 0.0).astype(F32)
    wide = jnp.dot(spread[...], owner, precision=lax.Precision.HIGHEST, preferred_element_type=F32)
    skip = wide[2 * rows : 2 * rows + 1]
    for req in range(requests):
        start = req * steps
        seq[0:history, :] = hist_ref[req].astype(F32)
        seq[history : history + steps, :] = inner_ref[start : start + steps, :]
        x_conv = conv_steps(seq, taps_ref[...], bias_ref[...], steps)
        kept_ref[req] = seq[steps : steps + history, :].astype(BF16)
        b_rows = pair_ref[0, start : start + steps, :]
        c_rows = pair_ref[1, start : start + steps, :]
        state = state_ref[req]
        c_high = c_rows.astype(BF16).astype(F32)
        rank[0:steps, 0:state_size] = c_high
        rank[steps : 2 * steps, 0:state_size] = c_rows - c_high
        rank[2 * steps :, 0:state_size] = jnp.zeros((rank.shape[0] - 2 * steps, state_size), F32)
        c_parts = rank[:, 0:state_size].astype(BF16)
        state_high = state.astype(BF16)
        state_low = (state - state_high.astype(F32)).astype(BF16)
        across = (((1,), (1,)), ((), ()))
        by_high = lax.dot_general(c_parts, state_high, across, preferred_element_type=F32)
        by_low = lax.dot_general(c_parts, state_low, across, preferred_element_type=F32)
        base[...] = by_high[0:steps] + by_high[steps : 2 * steps] + by_low[0:steps]
        taken = []
        fade = None
        for step_num in range(steps):
            row = start + step_num
            x_row = x_conv[step_num : step_num + 1]
            decay = wide[rows + row : rows + row + 1]
            fade = decay if fade is None else fade * decay
            taken = [(source, decay * value) for source, value in taken]
            taken.append((step_num, wide[row : row + 1] * x_row))
            y_row = fade * base[step_num : step_num + 1, :] + skip * x_row
            for source, value in taken:
                match = jnp.sum(
                    b_rows[source : source + 1] * c_rows[step_num : step_num + 1], axis=1, keepdims=True
                )
                y_row = y_row + match * value
            gated = y_row * silu(gate_ref[row : row + 1, :])
            gated_ref[row : row + 1, :] = gated
            square = jnp.sum(gated * gated, axis=1, keepdims=True)
            squares_ref[row : row + 1, :] = jnp.broadcast_to(square, (1, squares_ref.shape[1]))
        b_high = b_rows.astype(BF16).astype(F32)
        b_low = b_rows - b_high
        ones = jnp.ones((steps, state_size), F32)
        zeros = jnp.zeros((steps, state_size), F32)
        rank[0:steps, 0:state_size] = b_high
        rank[steps : 2 * steps, 0:state_size] = b_high
        rank[2 * steps : 3 * steps, 0:state_size] = b_low
        rank[3 * steps :, 0:state_size] = zeros
        rank[0:steps, state_size:] = zeros
        rank[steps : 2 * steps, state_size:] = zeros
        rank[2 * steps : 3 * steps, state_size:] = zeros
        rank[3 * steps :, state_size:] = ones
        right = rank[...].astype(BF16)
        for source, value in taken:
            high = value.astype(BF16).astype(F32)
            seq[source : source + 1, :] = high
            seq[steps + source : steps + source + 1, :] = value - high
            seq[2 * steps + source : 2 * steps + source + 1, :] = high
        fade_high = fade.astype(BF16).astype(F32)
        fade_mid = (fade - fade_high).astype(BF16).astype(F32)
        seq[3 * steps : 3 * steps + 1, :] = fade_high
        seq[3 * steps + 1 : 3 * steps + 2, :] = fade_mid
        seq[3 * steps + 2 : 3 * steps + 3, :] = fade - fade_high - fade_mid
        seq[3 * steps + 3 :, :] = jnp.zeros((seq.shape[0] - 3 * steps - 3, width), F32)
        left = seq[...].astype(BF16)
        both = lax.dot_general(left, right, (((0,), (0,)), ((), ())), preferred_element_type=F32)
        new_state_ref[req] = both[:, state_size:] * state + both[:, 0:state_size]


def normalise(group_width, gated_ref, squares_ref, gain_ref, out_ref, rows_two):
    rows, width = gated_ref.shape
    half = width // 2
    mean = (squares_ref[0] + squares_ref[1])[:, 0:1] / group_width
    normed = gated_ref[...] * lax.rsqrt(mean + EPSILON) * gain_ref[...]
    rows_two[0:rows, :] = normed[:, 0:half]
    rows_two[rows : 2 * rows, :] = normed[:, half:]
    block = rows_two[...].astype(BF16)
    for copy in range(out_ref.shape[0]):
        out_ref[copy] = block


def project_out(side_ref, in_ref, own_ref, other_ref, out_ref, first, second, sums):
    blocks, block_rows, half = in_ref.shape
    rows = block_rows // 2
    lanes = out_ref.shape[-1]
    flat = in_ref[...].reshape(blocks * block_rows, half)
    for weight_ref, side in ((own_ref, side_ref[0]), (other_ref, 1 - side_ref[0])):
        first[...] = jnp.dot(flat, weight_ref[0:half, :], preferred_element_type=F32)
        second[...] = jnp.dot(flat, weight_ref[half:, :], preferred_element_type=F32)
        for block in range(blocks):
            at = block * block_rows
            total = first[at : at + rows, :] + second[at + rows : at + block_rows, :]
            sums[block, side, 0:rows, :] = total[:, 0:lanes]
            sums[block, side, rows : 2 * rows, :] = total[:, lanes : 2 * lanes]
    out_ref[...] = sums[...].astype(BF16)


def shards(
    tokens,
    gate_inner_weight,
    step_weight,
    bc_weight,
    conv_inner,
    conv_groups,
    inner_taps,
    inner_bias,
    group_taps,
    group_bias,
    step_bias,
    log_decay,
    skip_gain,
    norm_gain,
    out_weight,
    ssm_state,
):
    steps, rows_head, features = tokens.shape
    requests, heads, head_size, state_size = ssm_state.shape
    width = heads * head_size
    req_count = REQ_COUNT
    rows = steps * requests
    sds = jax.ShapeDtypeStruct

    lanes = bc_weight.shape[1]
    chunk = width // SHARE
    with jax.named_scope("move_weights"):
        here = lax.axis_index(SHARE_AXIS)
        own_part, other_part = (
            lax.dynamic_slice(gate_inner_weight, (0, 0, side * chunk), (features, 2, chunk))
            for side in (here, 1 - here)
        )
        other_part = lax.ppermute(other_part, SHARE_AXIS, [(0, 1), (1, 0)])
        chunks = [part.reshape(features, 2 * chunk) for part in (own_part, other_part)]
        extra = jnp.concatenate(
            [bc_weight, step_weight, jnp.zeros((features, lanes - heads), BF16)], axis=1
        )

    with jax.named_scope("move_out_weight"):
        side = lax.axis_index(PAIR_AXIS)
        other_weight = lax.ppermute(out_weight, PAIR_AXIS, [(0, 1), (1, 0)])

    with jax.named_scope("gather_tokens"):
        own = call(
            copy_tokens,
            sds((SHARE * Y_SIZE, rows_head * steps, features), BF16),
            [pltpu.VMEM((rows_head * steps, features), F32)],
        )(jnp.transpose(tokens, (1, 0, 2)))
        gathered = lax.all_to_all(own, (SHARE_AXIS, "y"), 0, 0, tiled=True)
        gathered = lax.all_gather(gathered, "core", axis=0, tiled=False)

    with jax.named_scope("project"):
        tiles = 2 * chunk // lanes + 2
        message_rows = req_count * tiles * rows
        messages = call(
            project,
            sds((message_rows, lanes), BF16),
            [pltpu.VMEM((message_rows, lanes), F32)],
            [SCALARS] + [WHOLE] * 4 + [UNREAD],
        )(here.astype(jnp.int32).reshape(1), gathered, *chunks, extra, other_weight)
    with jax.named_scope("sum_req"):
        parts = lax.all_to_all(
            messages.reshape(req_count, tiles * rows, lanes), REQ_AXES, 0, 0, tiled=True
        )
        gate, inner, step, bc_conv, new_conv_groups = call(
            fold,
            (
                sds((rows, width), F32),
                sds((rows, width), F32),
                sds((rows, lanes), F32),
                sds((rows, lanes), F32),
                sds(conv_groups.shape, BF16),
            ),
            [pltpu.VMEM((8, lanes), F32)],
        )(parts, conv_groups, group_taps, group_bias[None])
    with jax.named_scope("scan"):
        pair = lax.all_gather(bc_conv, "core", axis=0, tiled=False)
        gated, squares, new_state, new_conv_inner = call(
            scan_steps,
            (
                sds((rows, width), F32),
                sds((rows, 128), F32),
                sds((requests, width, state_size), F32),
                sds(conv_inner.shape, BF16),
            ),
            [
                pltpu.VMEM((4 * steps, width), F32),
                pltpu.VMEM((32, heads), F32),
                pltpu.VMEM((4 * steps, 2 * state_size), F32),
                pltpu.VMEM((steps, width), F32),
            ],
        )(
            gate,
            inner,
            step,
            pair,
            conv_inner,
            inner_taps,
            inner_bias[None],
            step_bias[None],
            log_decay[None],
            skip_gain[None],
            ssm_state.reshape(requests, width, state_size),
        )
    with jax.named_scope("normalise"):
        squares_pair = lax.all_gather(squares, "core", axis=0, tiled=False)
        normed = call(
            functools.partial(normalise, CORE_SIZE * width),
            sds((REST, 2 * rows, width // 2), BF16),
            [pltpu.VMEM((2 * rows, width // 2), F32)],
        )(gated, squares_pair, norm_gain[None])
    with jax.named_scope("gather_normed"):
        some_rows = lax.all_to_all(normed, REST_AXES, 0, 0, tiled=True)
    with jax.named_scope("project_out"):
        out_columns = out_weight.shape[1]
        block = (REST, 2, 2 * rows, out_columns // 2)
        product = call(
            project_out,
            sds(block, BF16),
            [
                pltpu.VMEM((REST * 2 * rows, out_columns), F32),
                pltpu.VMEM((REST * 2 * rows, out_columns), F32),
                pltpu.VMEM(block, F32),
            ],
            [SCALARS] + [WHOLE] * 3,
        )(side.astype(jnp.int32).reshape(1), some_rows, out_weight, other_weight)
    with jax.named_scope("sum_head"):
        blocks = product.reshape((2 * REST,) + block[2:])
        blocks = lax.all_to_all(blocks, HEAD_AXES + (PAIR_AXIS,), 0, 0, tiled=True)
        mixed = call(sum_heads, sds((rows_head, steps, out_columns), BF16))(blocks)
        mixed = jnp.transpose(mixed, (1, 0, 2))
    return (mixed, new_state.reshape(ssm_state.shape), new_conv_inner, new_conv_groups)


def solution(mesh):
    head, req = HEAD_AXES, REQ_AXES
    split = Mesh(
        mesh.devices.reshape((Y_SIZE, CORE_SIZE) + (2,) * len(REQ_AXES)), HEAD_AXES + REQ_AXES
    )
    placed = (
        P(None, head, req),
        P(req, None, head),
        P(req, head),
        P(req, head),
        P(req, None, head),
        P(req, None, head),
        P(None, head),
        P(head),
        P(None, head),
        P(head),
        P(head),
        P(head),
        P(head),
        P(head),
        P(head, req),
        P(req, head, None, None),
    )
    return jax.shard_map(
        shards,
        mesh=split,
        in_specs=placed,
        out_specs=(
            P(None, head, req),
            P(req, head, None, None),
            P(req, None, head),
            P(req, None, head),
        ),
        check_vma=False,
    )
```

```python
import functools

import jax
import jax.numpy as jnp
from jax import lax
from jax.experimental import pallas as pl
from jax.experimental.pallas import tpu as pltpu
from jax.sharding import Mesh
from jax.sharding import PartitionSpec as P

EPSILON = 1e-05
F32 = jnp.float32
BF16 = jnp.bfloat16
Y_SIZE, CORE_SIZE = 8, 2
HEAD_AXES = ("y", "core")
REQ_AXES = ("x1", "x0", "z2", "z1", "z0")
REQ_COUNT = 32
SHARE_AXIS = "x0"
SHARE = 2
MEMBERS = [[16 * x1 + 8 * x0 + z for x1 in range(2) for z in range(8)] for x0 in range(SHARE)]
PAIR_AXIS = "z0"
REST_AXES = ("x1", "x0", "z2", "z1")
REST = 16
STEP_LANES, PACKED = 16, 6
VMEM_LIMIT = 40 * 1024 * 1024


def silu(value):
    return value / (1.0 + jnp.exp(-value))


WHOLE = pl.BlockSpec(memory_space=pltpu.VMEM)
SCALARS = pl.BlockSpec(memory_space=pltpu.SMEM)
UNREAD = pl.BlockSpec(memory_space=pl.ANY)


def call(body, out_shape, scratch=(), in_specs=None):
    places = {} if in_specs is None else {"in_specs": in_specs}
    return pl.pallas_call(
        body,
        out_shape=out_shape,
        out_specs=jax.tree.map(lambda _: WHOLE, out_shape),
        scratch_shapes=list(scratch),
        compiler_params=pltpu.CompilerParams(vmem_limit_bytes=VMEM_LIMIT),
        **places,
    )


def copy_tokens(in_ref, out_ref, flat):
    requests, steps, _ = in_ref.shape
    for req in range(requests):
        flat[req * steps : (req + 1) * steps, :] = in_ref[req].astype(F32)
    block = flat[...].astype(BF16)
    for copy in range(out_ref.shape[0]):
        out_ref[copy] = block


def sum_heads(in_ref, out_ref):
    requests, steps, _ = out_ref.shape
    lanes = in_ref.shape[2]
    half = requests // 2
    for side in range(2):
        total = in_ref[side].astype(F32)
        for part in range(2 + side, in_ref.shape[0], 2):
            total = total + in_ref[part].astype(F32)
        for req in range(half):
            left, right = req * steps, (half + req) * steps
            out_ref[side * half + req, :, 0:lanes] = total[left : left + steps].astype(BF16)
            out_ref[side * half + req, :, lanes:] = total[right : right + steps].astype(BF16)


def project(
    here_ref, _side, rows_ref, own_ref, other_ref, extra_ref, _low, _high, out_ref, messages
):
    cores, per_core, block_rows, features = rows_ref.shape
    y_count = per_core // SHARE
    rows = block_rows // 2
    lanes = out_ref.shape[1]
    lines = out_ref.shape[0] // REQ_COUNT
    tiles = lines // rows
    here = here_ref[0]
    count = y_count * block_rows
    row = lax.broadcasted_iota(jnp.int32, (count, lanes), 0)
    slot = lax.broadcasted_iota(jnp.int32, (count, lanes), 1) // STEP_LANES
    kept = lax.rem(row, PACKED) == slot
    line = lax.broadcasted_iota(jnp.int32, (count // PACKED, count), 0) * PACKED
    row = lax.broadcasted_iota(jnp.int32, (count // PACKED, count), 1)
    adder = jnp.where((row >= line) & (row < line + PACKED), 1.0, 0.0).astype(BF16)
    for core in range(cores):
        total = None
        for shift, weight_ref in enumerate((own_ref, other_ref)):
            source = 1 - here if shift else here
            block = rows_ref[core, pl.ds(source * y_count, y_count)]
            block = block.reshape(y_count * block_rows, features)
            part = jnp.dot(block, weight_ref[...], preferred_element_type=F32)
            total = part if total is None else total + part
            if shift == 0:
                extra = jnp.dot(block, extra_ref[...], preferred_element_type=F32)
        step = jnp.where(kept, extra[:, lanes:], 0.0).astype(BF16)
        step = jnp.dot(adder, step, preferred_element_type=F32)
        for y in range(y_count):
            for side in range(2):
                target = 2 * (y * cores + core) + side
                at = y * block_rows + side * rows
                for tile in range(tiles):
                    value, column = total, tile * lanes
                    if column >= total.shape[1]:
                        value, column = extra, column - total.shape[1]
                    to = target * lines + tile * rows
                    messages[to : to + rows, :] = value[at : at + rows, column : column + lanes]
                to, packed = target * lines + tiles * rows, rows // PACKED
                at = (2 * y + side) * packed
                messages[to : to + packed, :] = step[at : at + packed, :]
                messages[to + packed : (target + 1) * lines, :] = jnp.zeros(
                    (lines - tiles * rows - packed, lanes), F32
                )
    out_ref[...] = messages[...].astype(BF16)


def conv_steps(seq, taps, bias, steps):
    summed = taps[0:1, :] * seq[0:steps]
    for tap in range(1, taps.shape[0]):
        summed = summed + taps[tap : tap + 1, :] * seq[tap : tap + steps]
    return silu(summed + bias)


def fold(
    in_ref, hist_ref, taps_ref, bias_ref, gate_ref, inner_ref, step_ref, bc_ref, kept_ref, seq
):
    requests, history, lanes = hist_ref.shape
    rows = gate_ref.shape[0]
    steps = rows // requests
    chunk = gate_ref.shape[1] // SHARE
    tiles = chunk // lanes
    extra = None
    for share, members in enumerate(MEMBERS):
        total = in_ref[members[0]].astype(F32)
        for member in members[1:]:
            total = total + in_ref[member].astype(F32)
        rounded = total.astype(BF16).astype(F32)
        for tile in range(tiles):
            column = share * chunk + tile * lanes
            gate_ref[:, column : column + lanes] = rounded[tile * rows : (tile + 1) * rows]
            at = (tiles + tile) * rows
            inner_ref[:, column : column + lanes] = rounded[at : at + rows]
        part = total[2 * tiles * rows :]
        extra = part if extra is None else extra + part
    extra = extra.astype(BF16).astype(F32)
    for at in range(rows):
        line, lane = rows + at // PACKED, at % PACKED * STEP_LANES
        step_ref[at : at + 1, :] = extra[line : line + 1, lane : lane + STEP_LANES]
    for req in range(requests):
        seq[0:history, :] = hist_ref[req].astype(F32)
        seq[history : history + steps, :] = extra[req * steps : (req + 1) * steps]
        bc_ref[req * steps : (req + 1) * steps, :] = conv_steps(seq, taps_ref[...], bias_ref[...], steps)
        kept_ref[req] = seq[steps : steps + history, :].astype(BF16)


def scan_steps(
    gate_ref,
    inner_ref,
    step_ref,
    pair_ref,
    hist_ref,
    taps_ref,
    bias_ref,
    step_bias_ref,
    log_decay_ref,
    skip_ref,
    state_ref,
    gated_ref,
    squares_ref,
    new_state_ref,
    kept_ref,
    seq,
    spread,
    rank,
    base,
):
    requests, width, state_size = state_ref.shape
    heads = step_bias_ref.shape[1]
    history = hist_ref.shape[1]
    rows = gated_ref.shape[0]
    steps = rows // requests
    step = step_ref[...] + step_bias_ref[...]
    step_size = jnp.maximum(step, 0.0) + jnp.log1p(jnp.exp(-jnp.abs(step)))
    spread[0:rows, :] = step_size
    spread[rows : 2 * rows, :] = jnp.exp(-step_size * jnp.exp(log_decay_ref[...]))
    spread[2 * rows : 2 * rows + 1, :] = skip_ref[...]
    spread[2 * rows + 1 :, :] = jnp.zeros((spread.shape[0] - 2 * rows - 1, heads), F32)
    per_head = width // heads
    channel = lax.broadcasted_iota(jnp.int32, (heads, width), 1)
    low = lax.broadcasted_iota(jnp.int32, (heads, width), 0) * per_head
    owner = jnp.where((channel >= low) & (channel < low + per_head), 1.0, 0.0).astype(F32)
    wide = jnp.dot(spread[...], owner, precision=lax.Precision.HIGHEST, preferred_element_type=F32)
    skip = wide[2 * rows : 2 * rows + 1]
    for req in range(requests):
        start = req * steps
        seq[0:history, :] = hist_ref[req].astype(F32)
        seq[history : history + steps, :] = inner_ref[start : start + steps, :]
        x_conv = conv_steps(seq, taps_ref[...], bias_ref[...], steps)
        kept_ref[req] = seq[steps : steps + history, :].astype(BF16)
        b_rows = pair_ref[0, start : start + steps, :]
        c_rows = pair_ref[1, start : start + steps, :]
        state = state_ref[req]
        c_high = c_rows.astype(BF16).astype(F32)
        rank[0:steps, 0:state_size] = c_high
        rank[steps : 2 * steps, 0:state_size] = c_rows - c_high
        rank[2 * steps :, 0:state_size] = jnp.zeros((rank.shape[0] - 2 * steps, state_size), F32)
        c_parts = rank[:, 0:state_size].astype(BF16)
        state_high = state.astype(BF16)
        state_low = (state - state_high.astype(F32)).astype(BF16)
        across = (((1,), (1,)), ((), ()))
        by_high = lax.dot_general(c_parts, state_high, across, preferred_element_type=F32)
        by_low = lax.dot_general(c_parts, state_low, across, preferred_element_type=F32)
        base[...] = by_high[0:steps] + by_high[steps : 2 * steps] + by_low[0:steps]
        taken = []
        fade = None
        for step_num in range(steps):
            row = start + step_num
            x_row = x_conv[step_num : step_num + 1]
            decay = wide[rows + row : rows + row + 1]
            fade = decay if fade is None else fade * decay
            taken = [(source, decay * value) for source, value in taken]
            taken.append((step_num, wide[row : row + 1] * x_row))
            y_row = fade * base[step_num : step_num + 1, :] + skip * x_row
            for source, value in taken:
                match = jnp.sum(
                    b_rows[source : source + 1] * c_rows[step_num : step_num + 1], axis=1, keepdims=True
                )
                y_row = y_row + match * value
            gated = y_row * silu(gate_ref[row : row + 1, :])
            gated_ref[row : row + 1, :] = gated
            square = jnp.sum(gated * gated, axis=1, keepdims=True)
            squares_ref[row : row + 1, :] = jnp.broadcast_to(square, (1, squares_ref.shape[1]))
        b_high = b_rows.astype(BF16).astype(F32)
        b_low = b_rows - b_high
        ones = jnp.ones((steps, state_size), F32)
        zeros = jnp.zeros((steps, state_size), F32)
        rank[0:steps, 0:state_size] = b_high
        rank[steps : 2 * steps, 0:state_size] = b_high
        rank[2 * steps : 3 * steps, 0:state_size] = b_low
        rank[3 * steps :, 0:state_size] = zeros
        rank[0:steps, state_size:] = zeros
        rank[steps : 2 * steps, state_size:] = zeros
        rank[2 * steps : 3 * steps, state_size:] = zeros
        rank[3 * steps :, state_size:] = ones
        right = rank[...].astype(BF16)
        for source, value in taken:
            high = value.astype(BF16).astype(F32)
            seq[source : source + 1, :] = high
            seq[steps + source : steps + source + 1, :] = value - high
            seq[2 * steps + source : 2 * steps + source + 1, :] = high
        fade_high = fade.astype(BF16).astype(F32)
        fade_mid = (fade - fade_high).astype(BF16).astype(F32)
        seq[3 * steps : 3 * steps + 1, :] = fade_high
        seq[3 * steps + 1 : 3 * steps + 2, :] = fade_mid
        seq[3 * steps + 2 : 3 * steps + 3, :] = fade - fade_high - fade_mid
        seq[3 * steps + 3 :, :] = jnp.zeros((seq.shape[0] - 3 * steps - 3, width), F32)
        left = seq[...].astype(BF16)
        both = lax.dot_general(left, right, (((0,), (0,)), ((), ())), preferred_element_type=F32)
        new_state_ref[req] = both[:, state_size:] * state + both[:, 0:state_size]


def normalise(group_width, gated_ref, squares_ref, gain_ref, out_ref, rows_two):
    rows, width = gated_ref.shape
    half = width // 2
    mean = (squares_ref[0] + squares_ref[1])[:, 0:1] / group_width
    normed = gated_ref[...] * lax.rsqrt(mean + EPSILON) * gain_ref[...]
    rows_two[0:rows, :] = normed[:, 0:half]
    rows_two[rows : 2 * rows, :] = normed[:, half:]
    block = rows_two[...].astype(BF16)
    for copy in range(out_ref.shape[0]):
        out_ref[copy] = block


def project_out(side_ref, in_ref, own_ref, low_ref, high_ref, out_ref, first, second, sums):
    blocks, block_rows, half = in_ref.shape
    rows = block_rows // 2
    lanes = out_ref.shape[-1]
    flat = in_ref[...].reshape(blocks * block_rows, half)
    here = side_ref[0]
    for low, high, side in (
        (own_ref[0:half, :], own_ref[half:, :], here),
        (low_ref[...], high_ref[...], 1 - here),
    ):
        first[...] = jnp.dot(flat, low, preferred_element_type=F32)
        second[...] = jnp.dot(flat, high, preferred_element_type=F32)
        for block in range(blocks):
            at = block * block_rows
            total = first[at : at + rows, :] + second[at + rows : at + block_rows, :]
            sums[block, side, 0:rows, :] = total[:, 0:lanes]
            sums[block, side, rows : 2 * rows, :] = total[:, lanes : 2 * lanes]
    out_ref[...] = sums[...].astype(BF16)


def shards(
    tokens,
    gate_inner_weight,
    step_weight,
    bc_weight,
    conv_inner,
    conv_groups,
    inner_taps,
    inner_bias,
    group_taps,
    group_bias,
    step_bias,
    log_decay,
    skip_gain,
    norm_gain,
    out_weight,
    ssm_state,
):
    steps, rows_head, features = tokens.shape
    requests, heads, head_size, state_size = ssm_state.shape
    width = heads * head_size
    req_count = REQ_COUNT
    rows = steps * requests
    sds = jax.ShapeDtypeStruct

    lanes = bc_weight.shape[1]
    chunk = width // SHARE
    with jax.named_scope("move_weights"):
        here = lax.axis_index(SHARE_AXIS)
        own_part = lax.dynamic_slice(
            lax.optimization_barrier(gate_inner_weight),
            (0, 0, here * chunk),
            (features, 2, chunk),
        )
        other_part = lax.dynamic_slice(
            gate_inner_weight, (0, 0, (1 - here) * chunk), (features, 2, chunk)
        )
        other_part = lax.ppermute(other_part, SHARE_AXIS, [(0, 1), (1, 0)])
        chunks = [part.reshape(features, 2 * chunk) for part in (own_part, other_part)]
        extra = jnp.concatenate(
            [bc_weight] + [step_weight] * (lanes // heads), axis=1
        )

    with jax.named_scope("move_out_weight"):
        side = lax.axis_index(PAIR_AXIS).astype(jnp.int32).reshape(1)
        middle = out_weight.shape[0] // 2
        other_weights = [
            lax.ppermute(part, PAIR_AXIS, [(0, 1), (1, 0)])
            for part in (out_weight[:middle], out_weight[middle:])
        ]

    with jax.named_scope("gather_tokens"):
        own = call(
            copy_tokens,
            sds((SHARE * Y_SIZE, rows_head * steps, features), BF16),
            [pltpu.VMEM((rows_head * steps, features), F32)],
        )(jnp.transpose(tokens, (1, 0, 2)))
        gathered = lax.all_to_all(own, (SHARE_AXIS, "y"), 0, 0, tiled=True)
        gathered = lax.all_gather(gathered, "core", axis=0, tiled=False)

    with jax.named_scope("project"):
        lines = (2 * chunk // lanes + 1) * rows + rows // PACKED
        lines += -lines % 8
        message_rows = req_count * lines
        messages = call(
            project,
            sds((message_rows, lanes), BF16),
            [pltpu.VMEM((message_rows, lanes), F32)],
            [SCALARS] * 2 + [WHOLE] * 4 + [UNREAD] * 2,
        )(here.astype(jnp.int32).reshape(1), side, gathered, *chunks, extra, *other_weights)
    with jax.named_scope("sum_req"):
        parts = lax.all_to_all(
            messages.reshape(req_count, lines, lanes), REQ_AXES, 0, 0, tiled=True
        )
        gate, inner, step, bc_conv, new_conv_groups = call(
            fold,
            (
                sds((rows, width), F32),
                sds((rows, width), F32),
                sds((rows, heads), F32),
                sds((rows, lanes), F32),
                sds(conv_groups.shape, BF16),
            ),
            [pltpu.VMEM((8, lanes), F32)],
        )(parts, conv_groups, group_taps, group_bias[None])
    with jax.named_scope("scan"):
        pair = lax.all_gather(bc_conv, "core", axis=0, tiled=False)
        gated, squares, new_state, new_conv_inner = call(
            scan_steps,
            (
                sds((rows, width), F32),
                sds((rows, 128), F32),
                sds((requests, width, state_size), F32),
                sds(conv_inner.shape, BF16),
            ),
            [
                pltpu.VMEM((4 * steps, width), F32),
                pltpu.VMEM((32, heads), F32),
                pltpu.VMEM((4 * steps, 2 * state_size), F32),
                pltpu.VMEM((steps, width), F32),
            ],
        )(
            gate,
            inner,
            step,
            pair,
            conv_inner,
            inner_taps,
            inner_bias[None],
            step_bias[None],
            log_decay[None],
            skip_gain[None],
            ssm_state.reshape(requests, width, state_size),
        )
    with jax.named_scope("normalise"):
        squares_pair = lax.all_gather(squares, "core", axis=0, tiled=False)
        normed = call(
            functools.partial(normalise, CORE_SIZE * width),
            sds((REST, 2 * rows, width // 2), BF16),
            [pltpu.VMEM((2 * rows, width // 2), F32)],
        )(gated, squares_pair, norm_gain[None])
    with jax.named_scope("gather_normed"):
        some_rows = lax.all_to_all(normed, REST_AXES, 0, 0, tiled=True)
    with jax.named_scope("project_out"):
        out_columns = out_weight.shape[1]
        block = (REST, 2, 2 * rows, out_columns // 2)
        product = call(
            project_out,
            sds(block, BF16),
            [
                pltpu.VMEM((REST * 2 * rows, out_columns), F32),
                pltpu.VMEM((REST * 2 * rows, out_columns), F32),
                pltpu.VMEM(block, F32),
            ],
            [SCALARS] + [WHOLE] * 4,
        )(side, some_rows, out_weight, *other_weights)
    with jax.named_scope("sum_head"):
        blocks = product.reshape((2 * REST,) + block[2:])
        blocks = lax.all_to_all(blocks, HEAD_AXES + (PAIR_AXIS,), 0, 0, tiled=True)
        mixed = call(sum_heads, sds((rows_head, steps, out_columns), BF16))(blocks)
        mixed = jnp.transpose(mixed, (1, 0, 2))
    return (mixed, new_state.reshape(ssm_state.shape), new_conv_inner, new_conv_groups)


def solution(mesh):
    head, req = HEAD_AXES, REQ_AXES
    split = Mesh(
        mesh.devices.reshape((Y_SIZE, CORE_SIZE) + (2,) * len(REQ_AXES)), HEAD_AXES + REQ_AXES
    )
    placed = (
        P(None, head, req),
        P(req, None, head),
        P(req, head),
        P(req, head),
        P(req, None, head),
        P(req, None, head),
        P(None, head),
        P(head),
        P(None, head),
        P(head),
        P(head),
        P(head),
        P(head),
        P(head),
        P(head, req),
        P(req, head, None, None),
    )
    return jax.shard_map(
        shards,
        mesh=split,
        in_specs=placed,
        out_specs=(
            P(None, head, req),
            P(req, head, None, None),
            P(req, None, head),
            P(req, None, head),
        ),
        check_vma=False,
    )
```

```python
import functools

import jax
import jax.numpy as jnp
from jax import lax
from jax.experimental import pallas as pl
from jax.experimental.pallas import tpu as pltpu
from jax.sharding import Mesh
from jax.sharding import PartitionSpec as P

EPSILON = 1e-05
F32 = jnp.float32
BF16 = jnp.bfloat16
Y_SIZE, CORE_SIZE = 8, 2
HEAD_AXES = ("y", "core")
REQ_AXES = ("x1", "x0", "z2", "z1", "z0")
REQ_COUNT = 32
SHARE_AXIS = "x0"
SHARE = 2
MEMBERS = [[16 * x1 + 8 * x0 + z for x1 in range(2) for z in range(8)] for x0 in range(SHARE)]
PAIR_AXIS = "z0"
REST_AXES = ("x1", "x0", "z2", "z1")
REST = 16
STEP_LANES, PACKED = 16, 6
VMEM_LIMIT = 40 * 1024 * 1024


def silu(value):
    return value / (1.0 + jnp.exp(-value))


WHOLE = pl.BlockSpec(memory_space=pltpu.VMEM)
SCALARS = pl.BlockSpec(memory_space=pltpu.SMEM)
UNREAD = pl.BlockSpec(memory_space=pl.ANY)


def call(body, out_shape, scratch=(), in_specs=None):
    places = {} if in_specs is None else {"in_specs": in_specs}
    return pl.pallas_call(
        body,
        out_shape=out_shape,
        out_specs=jax.tree.map(lambda _: WHOLE, out_shape),
        scratch_shapes=list(scratch),
        compiler_params=pltpu.CompilerParams(vmem_limit_bytes=VMEM_LIMIT),
        **places,
    )


def copy_tokens(in_ref, out_ref, flat):
    requests, steps, _ = in_ref.shape
    for req in range(requests):
        flat[req * steps : (req + 1) * steps, :] = in_ref[req].astype(F32)
    block = flat[...].astype(BF16)
    for copy in range(out_ref.shape[0]):
        out_ref[copy] = block


def sum_heads(in_ref, out_ref):
    requests, steps, _ = out_ref.shape
    lanes = in_ref.shape[2]
    half = requests // 2
    for side in range(2):
        total = in_ref[side].astype(F32)
        for part in range(2 + side, in_ref.shape[0], 2):
            total = total + in_ref[part].astype(F32)
        for req in range(half):
            left, right = req * steps, (half + req) * steps
            out_ref[side * half + req, :, 0:lanes] = total[left : left + steps].astype(BF16)
            out_ref[side * half + req, :, lanes:] = total[right : right + steps].astype(BF16)


def project(
    here_ref, _side, rows_ref, own_ref, other_ref, extra_ref, _later, out_ref, messages
):
    cores, per_core, block_rows, features = rows_ref.shape
    y_count = per_core // SHARE
    rows = block_rows // 2
    lanes = out_ref.shape[1]
    lines = out_ref.shape[0] // REQ_COUNT
    tiles = lines // rows
    here = here_ref[0]
    count = y_count * block_rows
    row = lax.broadcasted_iota(jnp.int32, (count, lanes), 0)
    slot = lax.broadcasted_iota(jnp.int32, (count, lanes), 1) // STEP_LANES
    kept = lax.rem(row, PACKED) == slot
    line = lax.broadcasted_iota(jnp.int32, (count // PACKED, count), 0) * PACKED
    row = lax.broadcasted_iota(jnp.int32, (count // PACKED, count), 1)
    adder = jnp.where((row >= line) & (row < line + PACKED), 1.0, 0.0).astype(BF16)
    for core in range(cores):
        total = None
        for shift, weight_ref in enumerate((own_ref, other_ref)):
            source = 1 - here if shift else here
            block = rows_ref[core, pl.ds(source * y_count, y_count)]
            block = block.reshape(y_count * block_rows, features)
            part = jnp.dot(block, weight_ref[...], preferred_element_type=F32)
            total = part if total is None else total + part
            if shift == 0:
                extra = jnp.dot(block, extra_ref[...], preferred_element_type=F32)
        step = jnp.where(kept, extra[:, lanes:], 0.0).astype(BF16)
        step = jnp.dot(adder, step, preferred_element_type=F32)
        for y in range(y_count):
            for side in range(2):
                target = 2 * (y * cores + core) + side
                at = y * block_rows + side * rows
                for tile in range(tiles):
                    value, column = total, tile * lanes
                    if column >= total.shape[1]:
                        value, column = extra, column - total.shape[1]
                    to = target * lines + tile * rows
                    messages[to : to + rows, :] = value[at : at + rows, column : column + lanes]
                to, packed = target * lines + tiles * rows, rows // PACKED
                at = (2 * y + side) * packed
                messages[to : to + packed, :] = step[at : at + packed, :]
                messages[to + packed : (target + 1) * lines, :] = jnp.zeros(
                    (lines - tiles * rows - packed, lanes), F32
                )
    out_ref[...] = messages[...].astype(BF16)


def conv_steps(seq, taps, bias, steps):
    summed = taps[0:1, :] * seq[0:steps]
    for tap in range(1, taps.shape[0]):
        summed = summed + taps[tap : tap + 1, :] * seq[tap : tap + steps]
    return silu(summed + bias)


def fold(
    in_ref, hist_ref, taps_ref, bias_ref, gate_ref, inner_ref, step_ref, bc_ref, kept_ref, seq
):
    requests, history, lanes = hist_ref.shape
    rows = gate_ref.shape[0]
    steps = rows // requests
    chunk = gate_ref.shape[1] // SHARE
    tiles = chunk // lanes
    extra = None
    for share, members in enumerate(MEMBERS):
        total = in_ref[members[0]].astype(F32)
        for member in members[1:]:
            total = total + in_ref[member].astype(F32)
        rounded = total.astype(BF16).astype(F32)
        for tile in range(tiles):
            column = share * chunk + tile * lanes
            gate_ref[:, column : column + lanes] = rounded[tile * rows : (tile + 1) * rows]
            at = (tiles + tile) * rows
            inner_ref[:, column : column + lanes] = rounded[at : at + rows]
        part = total[2 * tiles * rows :]
        extra = part if extra is None else extra + part
    extra = extra.astype(BF16).astype(F32)
    for at in range(rows):
        line, lane = rows + at // PACKED, at % PACKED * STEP_LANES
        step_ref[at : at + 1, :] = extra[line : line + 1, lane : lane + STEP_LANES]
    for req in range(requests):
        seq[0:history, :] = hist_ref[req].astype(F32)
        seq[history : history + steps, :] = extra[req * steps : (req + 1) * steps]
        bc_ref[req * steps : (req + 1) * steps, :] = conv_steps(seq, taps_ref[...], bias_ref[...], steps)
        kept_ref[req] = seq[steps : steps + history, :].astype(BF16)


def scan_steps(
    gate_ref,
    inner_ref,
    step_ref,
    pair_ref,
    hist_ref,
    taps_ref,
    bias_ref,
    step_bias_ref,
    log_decay_ref,
    skip_ref,
    state_ref,
    gated_ref,
    squares_ref,
    new_state_ref,
    kept_ref,
    seq,
    spread,
    rank,
    base,
):
    requests, width, state_size = state_ref.shape
    heads = step_bias_ref.shape[1]
    history = hist_ref.shape[1]
    rows = gated_ref.shape[0]
    steps = rows // requests
    step = step_ref[...] + step_bias_ref[...]
    step_size = jnp.maximum(step, 0.0) + jnp.log1p(jnp.exp(-jnp.abs(step)))
    spread[0:rows, :] = step_size
    spread[rows : 2 * rows, :] = jnp.exp(-step_size * jnp.exp(log_decay_ref[...]))
    spread[2 * rows : 2 * rows + 1, :] = skip_ref[...]
    spread[2 * rows + 1 :, :] = jnp.zeros((spread.shape[0] - 2 * rows - 1, heads), F32)
    per_head = width // heads
    channel = lax.broadcasted_iota(jnp.int32, (heads, width), 1)
    low = lax.broadcasted_iota(jnp.int32, (heads, width), 0) * per_head
    owner = jnp.where((channel >= low) & (channel < low + per_head), 1.0, 0.0).astype(F32)
    wide = jnp.dot(spread[...], owner, precision=lax.Precision.HIGHEST, preferred_element_type=F32)
    skip = wide[2 * rows : 2 * rows + 1]
    for req in range(requests):
        start = req * steps
        seq[0:history, :] = hist_ref[req].astype(F32)
        seq[history : history + steps, :] = inner_ref[start : start + steps, :]
        x_conv = conv_steps(seq, taps_ref[...], bias_ref[...], steps)
        kept_ref[req] = seq[steps : steps + history, :].astype(BF16)
        b_rows = pair_ref[0, start : start + steps, :]
        c_rows = pair_ref[1, start : start + steps, :]
        state = state_ref[req]
        c_high = c_rows.astype(BF16).astype(F32)
        rank[0:steps, 0:state_size] = c_high
        rank[steps : 2 * steps, 0:state_size] = c_rows - c_high
        rank[2 * steps :, 0:state_size] = jnp.zeros((rank.shape[0] - 2 * steps, state_size), F32)
        c_parts = rank[:, 0:state_size].astype(BF16)
        state_high = state.astype(BF16)
        state_low = (state - state_high.astype(F32)).astype(BF16)
        across = (((1,), (1,)), ((), ()))
        by_high = lax.dot_general(c_parts, state_high, across, preferred_element_type=F32)
        by_low = lax.dot_general(c_parts, state_low, across, preferred_element_type=F32)
        base[...] = by_high[0:steps] + by_high[steps : 2 * steps] + by_low[0:steps]
        taken = []
        fade = None
        for step_num in range(steps):
            row = start + step_num
            x_row = x_conv[step_num : step_num + 1]
            decay = wide[rows + row : rows + row + 1]
            fade = decay if fade is None else fade * decay
            taken = [(source, decay * value) for source, value in taken]
            taken.append((step_num, wide[row : row + 1] * x_row))
            y_row = fade * base[step_num : step_num + 1, :] + skip * x_row
            for source, value in taken:
                match = jnp.sum(
                    b_rows[source : source + 1] * c_rows[step_num : step_num + 1], axis=1, keepdims=True
                )
                y_row = y_row + match * value
            gated = y_row * silu(gate_ref[row : row + 1, :])
            gated_ref[row : row + 1, :] = gated
            square = jnp.sum(gated * gated, axis=1, keepdims=True)
            squares_ref[row : row + 1, :] = jnp.broadcast_to(square, (1, squares_ref.shape[1]))
        b_high = b_rows.astype(BF16).astype(F32)
        b_low = b_rows - b_high
        ones = jnp.ones((steps, state_size), F32)
        zeros = jnp.zeros((steps, state_size), F32)
        rank[0:steps, 0:state_size] = b_high
        rank[steps : 2 * steps, 0:state_size] = b_high
        rank[2 * steps : 3 * steps, 0:state_size] = b_low
        rank[3 * steps :, 0:state_size] = zeros
        rank[0:steps, state_size:] = zeros
        rank[steps : 2 * steps, state_size:] = zeros
        rank[2 * steps : 3 * steps, state_size:] = zeros
        rank[3 * steps :, state_size:] = ones
        right = rank[...].astype(BF16)
        for source, value in taken:
            high = value.astype(BF16).astype(F32)
            seq[source : source + 1, :] = high
            seq[steps + source : steps + source + 1, :] = value - high
            seq[2 * steps + source : 2 * steps + source + 1, :] = high
        fade_high = fade.astype(BF16).astype(F32)
        fade_mid = (fade - fade_high).astype(BF16).astype(F32)
        seq[3 * steps : 3 * steps + 1, :] = fade_high
        seq[3 * steps + 1 : 3 * steps + 2, :] = fade_mid
        seq[3 * steps + 2 : 3 * steps + 3, :] = fade - fade_high - fade_mid
        seq[3 * steps + 3 :, :] = jnp.zeros((seq.shape[0] - 3 * steps - 3, width), F32)
        left = seq[...].astype(BF16)
        both = lax.dot_general(left, right, (((0,), (0,)), ((), ())), preferred_element_type=F32)
        new_state_ref[req] = both[:, state_size:] * state + both[:, 0:state_size]


def normalise(group_width, gated_ref, squares_ref, gain_ref, out_ref, rows_two):
    rows, width = gated_ref.shape
    half = width // 2
    mean = (squares_ref[0] + squares_ref[1])[:, 0:1] / group_width
    normed = gated_ref[...] * lax.rsqrt(mean + EPSILON) * gain_ref[...]
    rows_two[0:rows, :] = normed[:, 0:half]
    rows_two[rows : 2 * rows, :] = normed[:, half:]
    block = rows_two[...].astype(BF16)
    for copy in range(out_ref.shape[0]):
        out_ref[copy] = block


def project_out(side_ref, in_ref, own_ref, other_ref, out_ref, first, second, sums):
    blocks, block_rows, half = in_ref.shape
    rows = block_rows // 2
    lanes = out_ref.shape[-1]
    flat = in_ref[...].reshape(blocks * block_rows, half)
    for weight_ref, side in ((own_ref, side_ref[0]), (other_ref, 1 - side_ref[0])):
        first[...] = jnp.dot(flat, weight_ref[0:half, :], preferred_element_type=F32)
        second[...] = jnp.dot(flat, weight_ref[half:, :], preferred_element_type=F32)
        for block in range(blocks):
            at = block * block_rows
            total = first[at : at + rows, :] + second[at + rows : at + block_rows, :]
            sums[block, side, 0:rows, :] = total[:, 0:lanes]
            sums[block, side, rows : 2 * rows, :] = total[:, lanes : 2 * lanes]
    out_ref[...] = sums[...].astype(BF16)


def shards(
    tokens,
    gate_inner_weight,
    step_weight,
    bc_weight,
    conv_inner,
    conv_groups,
    inner_taps,
    inner_bias,
    group_taps,
    group_bias,
    step_bias,
    log_decay,
    skip_gain,
    norm_gain,
    out_weight,
    ssm_state,
):
    steps, rows_head, features = tokens.shape
    requests, heads, head_size, state_size = ssm_state.shape
    width = heads * head_size
    req_count = REQ_COUNT
    rows = steps * requests
    sds = jax.ShapeDtypeStruct

    lanes = bc_weight.shape[1]
    chunk = width // SHARE
    with jax.named_scope("move_weights"):
        here = lax.axis_index(SHARE_AXIS)
        own_part = lax.dynamic_slice(
            lax.optimization_barrier(gate_inner_weight),
            (0, 0, here * chunk),
            (features, 2, chunk),
        )
        other_part = lax.dynamic_slice(
            gate_inner_weight, (0, 0, (1 - here) * chunk), (features, 2, chunk)
        )
        other_part = lax.ppermute(other_part, SHARE_AXIS, [(0, 1), (1, 0)])
        chunks = [part.reshape(features, 2 * chunk) for part in (own_part, other_part)]
        extra = jnp.concatenate(
            [bc_weight] + [step_weight] * (lanes // heads), axis=1
        )

    with jax.named_scope("move_out_weight"):
        side = lax.axis_index(PAIR_AXIS).astype(jnp.int32).reshape(1)
        other_weight = lax.ppermute(out_weight, PAIR_AXIS, [(0, 1), (1, 0)])

    with jax.named_scope("gather_tokens"):
        own = call(
            copy_tokens,
            sds((SHARE * Y_SIZE, rows_head * steps, features), BF16),
            [pltpu.VMEM((rows_head * steps, features), F32)],
        )(jnp.transpose(tokens, (1, 0, 2)))
        gathered = lax.all_to_all(own, (SHARE_AXIS, "y"), 0, 0, tiled=True)
        gathered = lax.all_gather(gathered, "core", axis=0, tiled=False)

    with jax.named_scope("project"):
        lines = (2 * chunk // lanes + 1) * rows + rows // PACKED
        lines += -lines % 8
        message_rows = req_count * lines
        messages = call(
            project,
            sds((message_rows, lanes), BF16),
            [pltpu.VMEM((message_rows, lanes), F32)],
            [SCALARS] * 2 + [WHOLE] * 4 + [UNREAD],
        )(here.astype(jnp.int32).reshape(1), side, gathered, *chunks, extra, other_weight)
    with jax.named_scope("sum_req"):
        parts = lax.all_to_all(
            messages.reshape(req_count, lines, lanes), REQ_AXES, 0, 0, tiled=True
        )
        gate, inner, step, bc_conv, new_conv_groups = call(
            fold,
            (
                sds((rows, width), F32),
                sds((rows, width), F32),
                sds((rows, heads), F32),
                sds((rows, lanes), F32),
                sds(conv_groups.shape, BF16),
            ),
            [pltpu.VMEM((8, lanes), F32)],
        )(parts, conv_groups, group_taps, group_bias[None])
    with jax.named_scope("scan"):
        pair = lax.all_gather(bc_conv, "core", axis=0, tiled=False)
        gated, squares, new_state, new_conv_inner = call(
            scan_steps,
            (
                sds((rows, width), F32),
                sds((rows, 128), F32),
                sds((requests, width, state_size), F32),
                sds(conv_inner.shape, BF16),
            ),
            [
                pltpu.VMEM((4 * steps, width), F32),
                pltpu.VMEM((32, heads), F32),
                pltpu.VMEM((4 * steps, 2 * state_size), F32),
                pltpu.VMEM((steps, width), F32),
            ],
        )(
            gate,
            inner,
            step,
            pair,
            conv_inner,
            inner_taps,
            inner_bias[None],
            step_bias[None],
            log_decay[None],
            skip_gain[None],
            ssm_state.reshape(requests, width, state_size),
        )
    with jax.named_scope("normalise"):
        squares_pair = lax.all_gather(squares, "core", axis=0, tiled=False)
        normed = call(
            functools.partial(normalise, CORE_SIZE * width),
            sds((REST, 2 * rows, width // 2), BF16),
            [pltpu.VMEM((2 * rows, width // 2), F32)],
        )(gated, squares_pair, norm_gain[None])
    with jax.named_scope("gather_normed"):
        some_rows = lax.all_to_all(normed, REST_AXES, 0, 0, tiled=True)
    with jax.named_scope("project_out"):
        out_columns = out_weight.shape[1]
        block = (REST, 2, 2 * rows, out_columns // 2)
        product = call(
            project_out,
            sds(block, BF16),
            [
                pltpu.VMEM((REST * 2 * rows, out_columns), F32),
                pltpu.VMEM((REST * 2 * rows, out_columns), F32),
                pltpu.VMEM(block, F32),
            ],
            [SCALARS] + [WHOLE] * 3,
        )(side, some_rows, out_weight, other_weight)
    with jax.named_scope("sum_head"):
        blocks = product.reshape((2 * REST,) + block[2:])
        blocks = lax.all_to_all(blocks, HEAD_AXES + (PAIR_AXIS,), 0, 0, tiled=True)
        mixed = call(sum_heads, sds((rows_head, steps, out_columns), BF16))(blocks)
        mixed = jnp.transpose(mixed, (1, 0, 2))
    return (mixed, new_state.reshape(ssm_state.shape), new_conv_inner, new_conv_groups)


def solution(mesh):
    head, req = HEAD_AXES, REQ_AXES
    split = Mesh(
        mesh.devices.reshape((Y_SIZE, CORE_SIZE) + (2,) * len(REQ_AXES)), HEAD_AXES + REQ_AXES
    )
    placed = (
        P(None, head, req),
        P(req, None, head),
        P(req, head),
        P(req, head),
        P(req, None, head),
        P(req, None, head),
        P(None, head),
        P(head),
        P(None, head),
        P(head),
        P(head),
        P(head),
        P(head),
        P(head),
        P(head, req),
        P(req, head, None, None),
    )
    return jax.shard_map(
        shards,
        mesh=split,
        in_specs=placed,
        out_specs=(
            P(None, head, req),
            P(req, head, None, None),
            P(req, None, head),
            P(req, None, head),
        ),
        check_vma=False,
    )
```

```python
import functools

import jax
import jax.numpy as jnp
from jax import lax
from jax.experimental import pallas as pl
from jax.experimental.pallas import tpu as pltpu
from jax.sharding import Mesh
from jax.sharding import PartitionSpec as P

EPSILON = 1e-05
F32 = jnp.float32
BF16 = jnp.bfloat16
Y_SIZE, CORE_SIZE = 8, 2
HEAD_AXES = ("y", "core")
REQ_AXES = ("x1", "x0", "z2", "z1", "z0")
REQ_COUNT = 32
SHARE_AXIS = "x0"
SHARE = 2
MEMBERS = [[16 * x1 + 8 * x0 + z for x1 in range(2) for z in range(8)] for x0 in range(SHARE)]
PAIR_AXIS = "z0"
REST_AXES = ("x1", "x0", "z2", "z1")
REST = 16
STEP_LANES, PACKED = 16, 6
VMEM_LIMIT = 40 * 1024 * 1024


def silu(value):
    return value / (1.0 + jnp.exp(-value))


WHOLE = pl.BlockSpec(memory_space=pltpu.VMEM)
SCALARS = pl.BlockSpec(memory_space=pltpu.SMEM)
UNREAD = pl.BlockSpec(memory_space=pl.ANY)


def call(body, out_shape, scratch=(), in_specs=None):
    places = {} if in_specs is None else {"in_specs": in_specs}
    return pl.pallas_call(
        body,
        out_shape=out_shape,
        out_specs=jax.tree.map(lambda _: WHOLE, out_shape),
        scratch_shapes=list(scratch),
        compiler_params=pltpu.CompilerParams(vmem_limit_bytes=VMEM_LIMIT),
        **places,
    )


def copy_tokens(in_ref, out_ref, flat):
    requests, steps, _ = in_ref.shape
    for req in range(requests):
        flat[req * steps : (req + 1) * steps, :] = in_ref[req].astype(F32)
    block = flat[...].astype(BF16)
    for copy in range(out_ref.shape[0]):
        out_ref[copy] = block


def sum_heads(in_ref, out_ref):
    requests, steps, _ = out_ref.shape
    lanes = in_ref.shape[2]
    half = requests // 2
    for side in range(2):
        total = in_ref[side].astype(F32)
        for part in range(2 + side, in_ref.shape[0], 2):
            total = total + in_ref[part].astype(F32)
        for req in range(half):
            left, right = req * steps, (half + req) * steps
            out_ref[side * half + req, :, 0:lanes] = total[left : left + steps].astype(BF16)
            out_ref[side * half + req, :, lanes:] = total[right : right + steps].astype(BF16)


def project(
    here_ref, _side, rows_ref, own_ref, other_ref, extra_ref, _later, out_ref, messages
):
    cores, per_core, block_rows, features = rows_ref.shape
    y_count = per_core // SHARE
    rows = block_rows // 2
    lanes = out_ref.shape[1]
    lines = out_ref.shape[0] // REQ_COUNT
    tiles = lines // rows
    here = here_ref[0]
    count = y_count * block_rows
    row = lax.broadcasted_iota(jnp.int32, (count, lanes), 0)
    slot = lax.broadcasted_iota(jnp.int32, (count, lanes), 1) // STEP_LANES
    kept = lax.rem(row, PACKED) == slot
    line = lax.broadcasted_iota(jnp.int32, (count // PACKED, count), 0) * PACKED
    row = lax.broadcasted_iota(jnp.int32, (count // PACKED, count), 1)
    adder = jnp.where((row >= line) & (row < line + PACKED), 1.0, 0.0).astype(BF16)
    for core in range(cores):
        total = None
        for shift, weight_ref in enumerate((own_ref, other_ref)):
            source = 1 - here if shift else here
            block = rows_ref[core, pl.ds(source * y_count, y_count)]
            block = block.reshape(y_count * block_rows, features)
            part = jnp.dot(block, weight_ref[...], preferred_element_type=F32)
            total = part if total is None else total + part
            if shift == 0:
                extra = jnp.dot(block, extra_ref[...], preferred_element_type=F32)
        step = jnp.where(kept, extra[:, lanes:], 0.0).astype(BF16)
        step = jnp.dot(adder, step, preferred_element_type=F32)
        for y in range(y_count):
            for side in range(2):
                target = 2 * (y * cores + core) + side
                at = y * block_rows + side * rows
                for tile in range(tiles):
                    value, column = total, tile * lanes
                    if column >= total.shape[1]:
                        value, column = extra, column - total.shape[1]
                    to = target * lines + tile * rows
                    messages[to : to + rows, :] = value[at : at + rows, column : column + lanes]
                to, packed = target * lines + tiles * rows, rows // PACKED
                at = (2 * y + side) * packed
                messages[to : to + packed, :] = step[at : at + packed, :]
                messages[to + packed : (target + 1) * lines, :] = jnp.zeros(
                    (lines - tiles * rows - packed, lanes), F32
                )
    out_ref[...] = messages[...].astype(BF16)


def conv_steps(seq, taps, bias, steps):
    summed = taps[0:1, :] * seq[0:steps]
    for tap in range(1, taps.shape[0]):
        summed = summed + taps[tap : tap + 1, :] * seq[tap : tap + steps]
    return silu(summed + bias)


def fold(
    in_ref, hist_ref, taps_ref, bias_ref, gate_ref, inner_ref, step_ref, bc_ref, kept_ref, seq
):
    requests, history, lanes = hist_ref.shape
    rows = gate_ref.shape[0]
    steps = rows // requests
    chunk = gate_ref.shape[1] // SHARE
    tiles = chunk // lanes
    extra = None
    for share, members in enumerate(MEMBERS):
        total = in_ref[members[0]].astype(F32)
        for member in members[1:]:
            total = total + in_ref[member].astype(F32)
        rounded = total.astype(BF16).astype(F32)
        for tile in range(tiles):
            column = share * chunk + tile * lanes
            gate_ref[:, column : column + lanes] = rounded[tile * rows : (tile + 1) * rows]
            at = (tiles + tile) * rows
            inner_ref[:, column : column + lanes] = rounded[at : at + rows]
        part = total[2 * tiles * rows :]
        extra = part if extra is None else extra + part
    extra = extra.astype(BF16).astype(F32)
    for at in range(rows):
        line, lane = rows + at // PACKED, at % PACKED * STEP_LANES
        step_ref[at : at + 1, :] = extra[line : line + 1, lane : lane + STEP_LANES]
    for req in range(requests):
        seq[0:history, :] = hist_ref[req].astype(F32)
        seq[history : history + steps, :] = extra[req * steps : (req + 1) * steps]
        bc_ref[req * steps : (req + 1) * steps, :] = conv_steps(seq, taps_ref[...], bias_ref[...], steps)
        kept_ref[req] = seq[steps : steps + history, :].astype(BF16)


def scan_steps(
    gate_ref,
    inner_ref,
    step_ref,
    pair_ref,
    hist_ref,
    taps_ref,
    bias_ref,
    step_bias_ref,
    log_decay_ref,
    skip_ref,
    state_ref,
    gated_ref,
    squares_ref,
    new_state_ref,
    kept_ref,
    seq,
    spread,
    rank,
    base,
):
    requests, width, state_size = state_ref.shape
    heads = step_bias_ref.shape[1]
    history = hist_ref.shape[1]
    rows = gated_ref.shape[0]
    steps = rows // requests
    step = step_ref[...] + step_bias_ref[...]
    step_size = jnp.maximum(step, 0.0) + jnp.log1p(jnp.exp(-jnp.abs(step)))
    spread[0:rows, :] = step_size
    spread[rows : 2 * rows, :] = jnp.exp(-step_size * jnp.exp(log_decay_ref[...]))
    spread[2 * rows : 2 * rows + 1, :] = skip_ref[...]
    spread[2 * rows + 1 :, :] = jnp.zeros((spread.shape[0] - 2 * rows - 1, heads), F32)
    per_head = width // heads
    channel = lax.broadcasted_iota(jnp.int32, (heads, width), 1)
    low = lax.broadcasted_iota(jnp.int32, (heads, width), 0) * per_head
    owner = jnp.where((channel >= low) & (channel < low + per_head), 1.0, 0.0).astype(F32)
    wide = jnp.dot(spread[...], owner, precision=lax.Precision.HIGHEST, preferred_element_type=F32)
    skip = wide[2 * rows : 2 * rows + 1]
    for req in range(requests):
        start = req * steps
        seq[0:history, :] = hist_ref[req].astype(F32)
        seq[history : history + steps, :] = inner_ref[start : start + steps, :]
        x_conv = conv_steps(seq, taps_ref[...], bias_ref[...], steps)
        kept_ref[req] = seq[steps : steps + history, :].astype(BF16)
        b_rows = pair_ref[0, start : start + steps, :]
        c_rows = pair_ref[1, start : start + steps, :]
        state = state_ref[req]
        c_high = c_rows.astype(BF16).astype(F32)
        rank[0:steps, 0:state_size] = c_high
        rank[steps : 2 * steps, 0:state_size] = c_rows - c_high
        rank[2 * steps :, 0:state_size] = jnp.zeros((rank.shape[0] - 2 * steps, state_size), F32)
        c_parts = rank[:, 0:state_size].astype(BF16)
        state_high = state.astype(BF16)
        state_low = (state - state_high.astype(F32)).astype(BF16)
        across = (((1,), (1,)), ((), ()))
        by_high = lax.dot_general(c_parts, state_high, across, preferred_element_type=F32)
        by_low = lax.dot_general(c_parts, state_low, across, preferred_element_type=F32)
        base[...] = by_high[0:steps] + by_high[steps : 2 * steps] + by_low[0:steps]
        taken = []
        fade = None
        for step_num in range(steps):
            row = start + step_num
            x_row = x_conv[step_num : step_num + 1]
            decay = wide[rows + row : rows + row + 1]
            fade = decay if fade is None else fade * decay
            taken = [(source, decay * value) for source, value in taken]
            taken.append((step_num, wide[row : row + 1] * x_row))
            y_row = fade * base[step_num : step_num + 1, :] + skip * x_row
            for source, value in taken:
                match = jnp.sum(
                    b_rows[source : source + 1] * c_rows[step_num : step_num + 1], axis=1, keepdims=True
                )
                y_row = y_row + match * value
            gated = y_row * silu(gate_ref[row : row + 1, :])
            gated_ref[row : row + 1, :] = gated
            square = jnp.sum(gated * gated, axis=1, keepdims=True)
            squares_ref[row : row + 1, :] = jnp.broadcast_to(square, (1, squares_ref.shape[1]))
        b_high = b_rows.astype(BF16).astype(F32)
        b_low = b_rows - b_high
        ones = jnp.ones((steps, state_size), F32)
        zeros = jnp.zeros((steps, state_size), F32)
        rank[0:steps, 0:state_size] = b_high
        rank[steps : 2 * steps, 0:state_size] = b_high
        rank[2 * steps : 3 * steps, 0:state_size] = b_low
        rank[3 * steps :, 0:state_size] = zeros
        rank[0:steps, state_size:] = zeros
        rank[steps : 2 * steps, state_size:] = zeros
        rank[2 * steps : 3 * steps, state_size:] = zeros
        rank[3 * steps :, state_size:] = ones
        right = rank[...].astype(BF16)
        for source, value in taken:
            high = value.astype(BF16).astype(F32)
            seq[source : source + 1, :] = high
            seq[steps + source : steps + source + 1, :] = value - high
            seq[2 * steps + source : 2 * steps + source + 1, :] = high
        fade_high = fade.astype(BF16).astype(F32)
        fade_mid = (fade - fade_high).astype(BF16).astype(F32)
        seq[3 * steps : 3 * steps + 1, :] = fade_high
        seq[3 * steps + 1 : 3 * steps + 2, :] = fade_mid
        seq[3 * steps + 2 : 3 * steps + 3, :] = fade - fade_high - fade_mid
        seq[3 * steps + 3 :, :] = jnp.zeros((seq.shape[0] - 3 * steps - 3, width), F32)
        left = seq[...].astype(BF16)
        both = lax.dot_general(left, right, (((0,), (0,)), ((), ())), preferred_element_type=F32)
        new_state_ref[req] = both[:, state_size:] * state + both[:, 0:state_size]


def normalise(group_width, gated_ref, squares_ref, gain_ref, out_ref, rows_two):
    rows, width = gated_ref.shape
    half = width // 2
    mean = (squares_ref[0] + squares_ref[1])[:, 0:1] / group_width
    normed = gated_ref[...] * lax.rsqrt(mean + EPSILON) * gain_ref[...]
    rows_two[0:rows, :] = normed[:, 0:half]
    rows_two[rows : 2 * rows, :] = normed[:, half:]
    block = rows_two[...].astype(BF16)
    for copy in range(out_ref.shape[0]):
        out_ref[copy] = block


def project_out(side_ref, in_ref, own_ref, other_ref, out_ref, first, second, sums):
    blocks, block_rows, half = in_ref.shape
    rows = block_rows // 2
    lanes = out_ref.shape[-1]
    flat = in_ref[...].reshape(blocks * block_rows, half)
    for weight_ref, side in ((own_ref, side_ref[0]), (other_ref, 1 - side_ref[0])):
        first[...] = jnp.dot(flat, weight_ref[0:half, :], preferred_element_type=F32)
        second[...] = jnp.dot(flat, weight_ref[half:, :], preferred_element_type=F32)
        for block in range(blocks):
            at = block * block_rows
            total = first[at : at + rows, :] + second[at + rows : at + block_rows, :]
            sums[block, side, 0:rows, :] = total[:, 0:lanes]
            sums[block, side, rows : 2 * rows, :] = total[:, lanes : 2 * lanes]
    out_ref[...] = sums[...].astype(BF16)


def shards(
    tokens,
    gate_inner_weight,
    step_weight,
    bc_weight,
    conv_inner,
    conv_groups,
    inner_taps,
    inner_bias,
    group_taps,
    group_bias,
    step_bias,
    log_decay,
    skip_gain,
    norm_gain,
    out_weight,
    ssm_state,
):
    steps, rows_head, features = tokens.shape
    requests, heads, head_size, state_size = ssm_state.shape
    width = heads * head_size
    req_count = REQ_COUNT
    rows = steps * requests
    sds = jax.ShapeDtypeStruct

    lanes = bc_weight.shape[1]
    chunk = width // SHARE
    with jax.named_scope("gather_tokens"):
        own = call(
            copy_tokens,
            sds((SHARE * Y_SIZE, rows_head * steps, features), BF16),
            [pltpu.VMEM((rows_head * steps, features), F32)],
        )(jnp.transpose(tokens, (1, 0, 2)))
    with jax.named_scope("move_weights"):
        here = lax.axis_index(SHARE_AXIS)
        own_part = lax.dynamic_slice(
            lax.optimization_barrier(gate_inner_weight),
            (0, 0, here * chunk),
            (features, 2, chunk),
        )
        ahead, own = lax.optimization_barrier((gate_inner_weight, own))
        other_part = lax.dynamic_slice(
            ahead, (0, 0, (1 - here) * chunk), (features, 2, chunk)
        )
        other_part = lax.ppermute(other_part, SHARE_AXIS, [(0, 1), (1, 0)])
        chunks = [part.reshape(features, 2 * chunk) for part in (own_part, other_part)]
        extra = jnp.concatenate(
            [bc_weight] + [step_weight] * (lanes // heads), axis=1
        )

    with jax.named_scope("move_out_weight"):
        side = lax.axis_index(PAIR_AXIS).astype(jnp.int32).reshape(1)
        other_weight = lax.ppermute(out_weight, PAIR_AXIS, [(0, 1), (1, 0)])

    with jax.named_scope("gather_tokens"):
        gathered = lax.all_to_all(own, (SHARE_AXIS, "y"), 0, 0, tiled=True)
        gathered = lax.all_gather(gathered, "core", axis=0, tiled=False)

    with jax.named_scope("project"):
        lines = (2 * chunk // lanes + 1) * rows + rows // PACKED
        lines += -lines % 8
        message_rows = req_count * lines
        messages = call(
            project,
            sds((message_rows, lanes), BF16),
            [pltpu.VMEM((message_rows, lanes), F32)],
            [SCALARS] * 2 + [WHOLE] * 4 + [UNREAD],
        )(here.astype(jnp.int32).reshape(1), side, gathered, *chunks, extra, other_weight)
    with jax.named_scope("sum_req"):
        parts = lax.all_to_all(
            messages.reshape(req_count, lines, lanes), REQ_AXES, 0, 0, tiled=True
        )
        gate, inner, step, bc_conv, new_conv_groups = call(
            fold,
            (
                sds((rows, width), F32),
                sds((rows, width), F32),
                sds((rows, heads), F32),
                sds((rows, lanes), F32),
                sds(conv_groups.shape, BF16),
            ),
            [pltpu.VMEM((8, lanes), F32)],
        )(parts, conv_groups, group_taps, group_bias[None])
    with jax.named_scope("scan"):
        pair = lax.all_gather(bc_conv, "core", axis=0, tiled=False)
        gated, squares, new_state, new_conv_inner = call(
            scan_steps,
            (
                sds((rows, width), F32),
                sds((rows, 128), F32),
                sds((requests, width, state_size), F32),
                sds(conv_inner.shape, BF16),
            ),
            [
                pltpu.VMEM((4 * steps, width), F32),
                pltpu.VMEM((32, heads), F32),
                pltpu.VMEM((4 * steps, 2 * state_size), F32),
                pltpu.VMEM((steps, width), F32),
            ],
        )(
            gate,
            inner,
            step,
            pair,
            conv_inner,
            inner_taps,
            inner_bias[None],
            step_bias[None],
            log_decay[None],
            skip_gain[None],
            ssm_state.reshape(requests, width, state_size),
        )
    with jax.named_scope("normalise"):
        squares_pair = lax.all_gather(squares, "core", axis=0, tiled=False)
        normed = call(
            functools.partial(normalise, CORE_SIZE * width),
            sds((REST, 2 * rows, width // 2), BF16),
            [pltpu.VMEM((2 * rows, width // 2), F32)],
        )(gated, squares_pair, norm_gain[None])
    with jax.named_scope("gather_normed"):
        some_rows = lax.all_to_all(normed, REST_AXES, 0, 0, tiled=True)
    with jax.named_scope("project_out"):
        out_columns = out_weight.shape[1]
        block = (REST, 2, 2 * rows, out_columns // 2)
        product = call(
            project_out,
            sds(block, BF16),
            [
                pltpu.VMEM((REST * 2 * rows, out_columns), F32),
                pltpu.VMEM((REST * 2 * rows, out_columns), F32),
                pltpu.VMEM(block, F32),
            ],
            [SCALARS] + [WHOLE] * 3,
        )(side, some_rows, out_weight, other_weight)
    with jax.named_scope("sum_head"):
        blocks = product.reshape((2 * REST,) + block[2:])
        blocks = lax.all_to_all(blocks, HEAD_AXES + (PAIR_AXIS,), 0, 0, tiled=True)
        mixed = call(sum_heads, sds((rows_head, steps, out_columns), BF16))(blocks)
        mixed = jnp.transpose(mixed, (1, 0, 2))
    return (mixed, new_state.reshape(ssm_state.shape), new_conv_inner, new_conv_groups)


def solution(mesh):
    head, req = HEAD_AXES, REQ_AXES
    split = Mesh(
        mesh.devices.reshape((Y_SIZE, CORE_SIZE) + (2,) * len(REQ_AXES)), HEAD_AXES + REQ_AXES
    )
    placed = (
        P(None, head, req),
        P(req, None, head),
        P(req, head),
        P(req, head),
        P(req, None, head),
        P(req, None, head),
        P(None, head),
        P(head),
        P(None, head),
        P(head),
        P(head),
        P(head),
        P(head),
        P(head),
        P(head, req),
        P(req, head, None, None),
    )
    return jax.shard_map(
        shards,
        mesh=split,
        in_specs=placed,
        out_specs=(
            P(None, head, req),
            P(req, head, None, None),
            P(req, None, head),
            P(req, None, head),
        ),
        check_vma=False,
    )
```
